32 devices in a mesh: narrow: 4 (over y, x), wide: 8 (over z, core).
Axes of the slice: x: 2, y: 2, z: 4, core: 2. Of those that a mesh axis runs over, the one named last changes fastest.
Arguments:
- tokens: bfloat16 [128, 496, 768], P(('narrow', 'wide')), may hold values from -6 to 6
- patch_order: int32 [128, 496], P(('narrow', 'wide')), may hold values from 0 to 495, each once within a row
- visible: int32 [128], P(('narrow', 'wide')), may hold values from 1 to 128, 12288 in all
- query_weight: bfloat16 [768, 768], P('wide'), may hold values from -0.21875 to 0.21875
- key_weight: bfloat16 [768, 768], P('wide'), may hold values from -0.21875 to 0.21875
- value_weight: bfloat16 [768, 768], P('wide'), may hold values from -0.21875 to 0.21875
- out_weight: bfloat16 [768, 768], P('wide'), may hold values from -1.75 to 1.75
- up_weight: bfloat16 [768, 3072], P('wide'), may hold values from -0.21875 to 0.21875
- down_weight: bfloat16 [3072, 768], P('wide'), may hold values from -0.21875 to 0.21875
- query_bias: bfloat16 [768], P('wide'), may hold values from -1.796875 to 1.796875
- value_bias: bfloat16 [768], P('wide'), may hold values from -1.796875 to 1.796875
- out_bias: bfloat16 [768], P('wide'), may hold values from -1.796875 to 1.796875
- up_bias: bfloat16 [3072], P('wide'), may hold values from -1.796875 to 1.796875
- down_bias: bfloat16 [768], P('wide'), may hold values from -1.796875 to 1.796875
- first_gain: bfloat16 [768], P('wide'), may hold values from 0.5 to 1.5
- first_shift: bfloat16 [768], P('wide'), may hold values from -1.796875 to 1.796875
- second_gain: bfloat16 [768], P('wide'), may hold values from 0.5 to 1.5
- second_shift: bfloat16 [768], P('wide'), may hold values from -1.796875 to 1.796875
- bias_table: bfloat16 [320, 12], P('wide'), may hold values from -5 to 5
- gate_weight: float32 [64, 8], replicated, may hold values from -0.75 to 0.75
- gate_bias: float32 [8], replicated, may hold values from -2.5 to 2.5
- gate_scale: float32 [12], replicated, may hold values from 0.5 to 2
- cotangent: bfloat16 [128, 128, 768], P(('narrow', 'wide')), may hold values from -6 to 6
Outputs:
- output: bfloat16 [128, 128, 768], P(('narrow', 'wide'))
- tokens_grad: bfloat16 [128, 496, 768], P(('narrow', 'wide'))
- query_weight_grad: float32 [768, 768], P('wide')
- key_weight_grad: float32 [768, 768], P('wide')
- value_weight_grad: float32 [768, 768], P('wide')
- out_weight_grad: float32 [768, 768], P('wide')
- up_weight_grad: float32 [768, 3072], P('wide')
- down_weight_grad: float32 [3072, 768], P('wide')
- query_bias_grad: float32 [768], P('wide')
- value_bias_grad: float32 [768], P('wide')
- out_bias_grad: float32 [768], P('wide')
- up_bias_grad: float32 [3072], P('wide')
- down_bias_grad: float32 [768], P('wide')
- first_gain_grad: float32 [768], P('wide')
- first_shift_grad: float32 [768], P('wide')
- second_gain_grad: float32 [768], P('wide')
- second_shift_grad: float32 [768], P('wide')
- bias_table_grad: float32 [320, 12], P('wide')
- gate_weight_grad: float32 [64, 8], replicated
- gate_bias_grad: float32 [8], replicated
- gate_scale_grad: float32 [12], replicated
The draws below stay inside these ranges and needn't reach their ends.
Inputs may be any that keep to these rules, and one draw needn't show every extreme that they name: Each row of patch_order names every patch of a clip once. The most visible patches of a clip is exactly 128 in every draw.
All inputs are finite; a program needn't handle non-finite values. No bound on the sum of `visible` on one device may be relied on, other than what follows from the above.
Results may differ from the reference program's by a relative error of at most 0.023.
Values may be sent and summed in bfloat16 or wider, within the bound.
No kernel may reach another device: no remote copies, remote signals or barrier semaphores. Data moves between devices by JAX's collectives and lax.ppermute only.
A program may use at most 192 MiB of HBM per device.

```python
import math
import jax
import jax.numpy as jnp
import numpy as np
from jax import lax

D = 768
HEADS = 12
HEAD_DIM = 64
FF = 3072
NUM_BUCKETS = 320
PATCHES = 496
VIS = 128
CLIPS = 128


def block_levels(key, extent, shards, least, high):
    def one(dim, blocks):
        draws = jax.random.uniform(jax.random.fold_in(jax.random.fold_in(key, 6), dim), (blocks,), jnp.float32, least / len(shards), high / len(shards))
        return jnp.repeat(jnp.exp(draws), extent[dim] // blocks).reshape((-1,) + (1,) * (len(extent) - dim - 1))

    level = one(*shards[0])
    for cut in shards[1:]:
        level = level * one(*cut)
    return level


def split_up(number_of, total, reach, lean):
    loads = [(1 << 20) // math.isqrt(rank ** lean) + 1 for rank in range(2, number_of + 1)]
    rest, counts = total - reach - (number_of - 1), [1] * (number_of - 1)
    while rest > 0:
        free = [i for i in range(number_of - 1) if counts[i] < reach]
        mass, remaining = sum([loads[i] for i in free]), rest
        for i in free:
            more = min(reach - counts[i], max(1, remaining * loads[i] // mass), rest)
            counts[i] = counts[i] + more
            rest = rest - more
    return np.array([reach] + counts)


def ragged(own_key, number_of, total, reach, slope):
    if number_of == 2:
        one = jax.random.randint(own_key, (), max(1, total - reach), min(reach, total - 1) + 1)
        return jnp.stack([one, total - one])
    sizes = jnp.asarray(split_up(number_of, total, reach, slope), jnp.int32)
    pairs = (number_of - 1) // 2
    donor, taker = sizes[1:1 + 2 * pairs:2], sizes[2:2 + 2 * pairs:2]
    room = jnp.minimum(donor - 1, reach - taker)
    passed = jax.random.randint(jax.random.fold_in(own_key, 1), (pairs,), 0, 1 << 20) % (room + 1)
    sizes = sizes.at[1:1 + 2 * pairs:2].set(donor - passed).at[2:2 + 2 * pairs:2].set(taker + passed)
    return sizes[jax.random.permutation(jax.random.fold_in(own_key, 2), number_of)]


def centred(own_key, dims, width, limit, shards=(), kind=jnp.bfloat16):
    entries = jax.random.normal(own_key, dims, jnp.float32) * width
    if len(shards) > 0:
        entries = block_levels(own_key, dims, shards, -0.22, 0.18) * entries
    return jnp.clip(entries, min=-limit, max=limit).astype(kind)


def setup_inputs(seed: int = 0) -> dict:
    seeds = jax.random.split(jax.random.key(seed), 24)
    tokens = centred(seeds[0], (CLIPS, PATCHES, D), 1.0, 6.0, ((0, 32),))
    patch_order = jax.vmap(lambda own: jax.random.permutation(own, PATCHES))(jax.random.split(seeds[1], CLIPS)).reshape((CLIPS, PATCHES)).astype(jnp.int32)
    visible = ragged(seeds[2], CLIPS, CLIPS * VIS * 3 // 4, VIS, 1).astype(jnp.int32)
    query_weight = centred(seeds[3], (D, D), D ** -0.5, 0.21875, ((0, 8),))
    key_weight = centred(seeds[4], (D, D), D ** -0.5, 0.21875, ((0, 8),))
    value_weight = centred(seeds[5], (D, D), D ** -0.5, 0.21875, ((0, 8),))
    out_weight = centred(seeds[6], (D, D), (D // 64) ** -0.5, 1.75, ((0, 8),))
    up_weight = centred(seeds[7], (D, FF), D ** -0.5, 0.21875, ((0, 8),))
    down_weight = centred(seeds[8], (FF, D), (FF // 4) ** -0.5, 0.21875, ((0, 8),))
    query_bias = centred(seeds[9], (D,), 0.3, 1.796875, ((0, 8),))
    value_bias = centred(seeds[10], (D,), 0.3, 1.796875, ((0, 8),))
    out_bias = centred(seeds[11], (D,), 0.3, 1.796875, ((0, 8),))
    up_bias = centred(seeds[12], (FF,), 0.3, 1.796875, ((0, 8),))
    down_bias = centred(seeds[13], (D,), 0.3, 1.796875, ((0, 8),))
    first_gain = jnp.clip(1.0 + 0.1 * jax.random.normal(seeds[14], (D,), jnp.float32), 0.5, 1.5).astype(jnp.bfloat16)
    first_shift = centred(seeds[15], (D,), 0.3, 1.796875, ((0, 8),))
    second_gain = jnp.clip(1.0 + 0.1 * jax.random.normal(seeds[16], (D,), jnp.float32), 0.5, 1.5).astype(jnp.bfloat16)
    second_shift = centred(seeds[17], (D,), 0.3, 1.796875, ((0, 8),))
    bias_table = centred(seeds[18], (NUM_BUCKETS, HEADS), 1.0, 5.0, ((0, 8),))
    gate_weight = centred(seeds[19], (HEAD_DIM, 8), HEAD_DIM ** -0.5, 0.75, (), jnp.float32)
    gate_bias = centred(seeds[20], (8,), 0.5, 2.5, (), jnp.float32)
    gate_scale = jnp.clip(jax.random.uniform(seeds[21], (HEADS,), jnp.float32, 0.5, 2.0), 0.5, 2.0)
    cotangent = centred(seeds[22], (CLIPS, VIS, D), 1.0, 6.0, ((0, 32),))
    return dict(tokens=tokens, patch_order=patch_order, visible=visible, query_weight=query_weight, key_weight=key_weight, value_weight=value_weight, out_weight=out_weight, up_weight=up_weight, down_weight=down_weight, query_bias=query_bias, value_bias=value_bias, out_bias=out_bias, up_bias=up_bias, down_bias=down_bias, first_gain=first_gain, first_shift=first_shift, second_gain=second_gain, second_shift=second_shift, bias_table=bias_table, gate_weight=gate_weight, gate_bias=gate_bias, gate_scale=gate_scale, cotangent=cotangent)


highest = lax.Precision.HIGHEST
deep_alpha = math.pow(24.0, 0.25)
norm_eps = 1e-05

@jax.custom_vjp
def low(v):
    return lax.optimization_barrier(v.astype(jnp.bfloat16)).astype(jnp.float32)

@jax.custom_vjp
def low_back(v):
    return v

def low_keep(v):
    return (low(v), None)

def low_pass(kept, grad):
    return (grad,)

def back_keep(v):
    return (v, None)

def back_low(kept, grad):
    return (low(grad),)
low.defvjp(low_keep, low_pass)
low_back.defvjp(back_keep, back_low)

def bucket_table(patch_count):
    relative = np.arange(1 - patch_count, patch_count)
    distance = np.abs(relative)
    ratio = np.log(np.maximum(distance, 1) / 80.0) / math.log(10.0)
    beyond = np.minimum(80 + np.floor(ratio * 80.0).astype(np.int64), 159)
    return np.where(relative > 0, 160, 0) + np.where(distance < 80, distance, beyond)

def layer_norm(values, gain, shift):
    center = values - lax.optimization_barrier(jnp.mean(values, -1, keepdims=True))
    spread = lax.optimization_barrier(jnp.mean(center * center, -1, keepdims=True))
    return center * lax.rsqrt(spread + norm_eps) * gain + shift

def dense(inputs, matrix):
    return jnp.einsum('cvd,df->cvf', inputs, matrix, precision=highest)

def forward(inputs, order_block, visible_block, query_weight, key_weight, value_weight, out_weight, up_weight, down_weight, query_bias, value_bias, out_bias, up_bias, down_bias, first_gain, first_shift, second_gain, second_shift, bias_table, gate_weight, gate_bias, gate_scale):
    group_size = inputs.shape[0]
    slots = order_block[:, :VIS]
    row_live = jnp.arange(VIS, dtype=jnp.int32)[None, :] < visible_block[:, None]
    match = (slots[:, :, None] == jnp.arange(PATCHES, dtype=jnp.int32)[None, None, :]) & row_live[:, :, None]
    select = jnp.where(match, 1.0, 0.0).astype(jnp.float32)
    picked = low_back(jnp.einsum('cvp,cpd->cvd', select, inputs, precision=highest))
    head_shape = (group_size, VIS, HEADS, HEAD_DIM)
    query = low(low_back(dense(picked, query_weight) + query_bias)).reshape(head_shape)
    key_rows = low(low_back(dense(picked, key_weight))).reshape(head_shape)
    value_rows = low(low_back(dense(picked, value_weight) + value_bias)).reshape(head_shape)
    scores = jnp.einsum('cihe,cjhe->chij', query, key_rows, precision=highest) * HEAD_DIM ** (-0.5)
    logits = jnp.einsum('cihe,ef->cihf', picked.reshape(head_shape), gate_weight, precision=highest) + gate_bias
    gate_first = jax.nn.sigmoid(lax.optimization_barrier(jnp.sum(logits[..., :4], -1)))
    gate_second = jax.nn.sigmoid(lax.optimization_barrier(jnp.sum(logits[..., 4:], -1)))
    gate_value = gate_first * (gate_second * gate_scale - 1.0) + 2.0
    table = jnp.asarray(bucket_table(PATCHES), dtype=jnp.int32)
    distance_bias = bias_table[table]
    offsets = slots[:, None, :] - slots[:, :, None] + (PATCHES - 1)
    position = jnp.transpose(jnp.take(distance_bias.T, offsets, axis=1), (1, 0, 2, 3))
    scores = scores + jnp.transpose(gate_value, (0, 2, 1))[..., None] * position
    scores = low_back(jnp.where(row_live[:, None, None, :], scores, -1000000000.0))
    attention_weights = jax.nn.softmax(scores, axis=-1)
    head_mixed = jnp.einsum('chij,cjhe->cihe', low(attention_weights), value_rows, precision=highest)
    head_mixed = low(low_back(head_mixed.reshape(group_size, VIS, D)))
    attended = low_back(dense(head_mixed, out_weight) + out_bias)
    normed = layer_norm(deep_alpha * picked + attended, first_gain, first_shift)
    hidden = low_back(dense(low(normed), up_weight) + up_bias)
    activated = low(jax.nn.gelu(hidden, approximate=False))
    branch = low_back(dense(activated, down_weight) + down_bias)
    return layer_norm(deep_alpha * normed + branch, second_gain, second_shift)

def reference(tokens, patch_order, visible, query_weight, key_weight, value_weight, out_weight, up_weight, down_weight, query_bias, value_bias, out_bias, up_bias, down_bias, first_gain, first_shift, second_gain, second_shift, bias_table, gate_weight, gate_bias, gate_scale, cotangent):
    params = tuple((param.astype(jnp.float32) for param in (query_weight, key_weight, value_weight, out_weight, up_weight, down_weight, query_bias, value_bias, out_bias, up_bias, down_bias, first_gain, first_shift, second_gain, second_shift, bias_table, gate_weight, gate_bias, gate_scale)))
    group_count = CLIPS // 32
    token_blocks = tokens.astype(jnp.float32).reshape(group_count, 32, PATCHES, D)
    order_blocks = patch_order.reshape(group_count, 32, PATCHES)
    visible_blocks = visible.reshape(group_count, 32)
    cot_blocks = cotangent.astype(jnp.float32).reshape(group_count, 32, VIS, D)

    def step(totals, block):
        token_block, order_block, visible_block, cot_block = block

        def layer(inputs, *weights):
            return forward(inputs, order_block, visible_block, *weights)
        result, pull = jax.vjp(layer, token_block, *params)
        row_live = (jnp.arange(VIS, dtype=jnp.int32)[None, :] < visible_block[:, None]).astype(jnp.float32)[:, :, None]
        grads = pull(cot_block * row_live)
        totals = tuple((total + update for total, update in zip(totals, grads[1:])))
        return (totals, ((result * row_live).astype(jnp.bfloat16), grads[0].astype(jnp.bfloat16)))
    totals, (outputs, token_grads) = lax.scan(step, tuple((jnp.zeros_like(param) for param in params)), (token_blocks, order_blocks, visible_blocks, cot_blocks))
    return (outputs.reshape(CLIPS, VIS, D), token_grads.reshape(CLIPS, PATCHES, D), totals[0], totals[1], totals[2], totals[3], totals[4], totals[5], totals[6], totals[7], totals[8], totals[9], totals[10], totals[11], totals[12], totals[13], totals[14], totals[15], totals[16], totals[17], totals[18])
```

```python
from functools import partial
import math

import jax
import jax.numpy as jnp
import numpy as np
from jax import lax
from jax.experimental import pallas as pl
from jax.experimental.pallas import tpu as pltpu
from jax.sharding import PartitionSpec as P

NUM_BUCKETS = 320
SPAN = 512
SPARE = 4
MOST = 51
HIGHEST = lax.Precision.HIGHEST
ALPHA = math.pow(24.0, 0.25)
EPS = 1e-05
F32 = jnp.float32
BF16 = jnp.bfloat16
NN = (((1,), (0,)), ((), ()))
NT = (((1,), (1,)), ((), ()))
TN = (((0,), (0,)), ((), ()))


def dot(a, b, dims=NN, precision=None):
    return lax.dot_general(a, b, dims, precision=precision, preferred_element_type=F32)


def params(need=0, *semantics):
    extra = dict(dimension_semantics=semantics) if semantics else {}
    need = need if need > 50 else min(need + SPARE, MOST) if need else MOST
    return pltpu.CompilerParams(vmem_limit_bytes=need * 1024 * 1024, **extra)


def size_of(x):
    shape = list(x.shape)
    shape[-1] = -(-shape[-1] // 128) * 128
    if len(shape) > 1:
        shape[-2] = -(-shape[-2] // 8) * 8
    return math.prod(shape) * jnp.dtype(x.dtype).itemsize


def cost(us):
    return pl.CostEstimate(
        flops=int(us * 1e10), bytes_accessed=int(us * 3.5e7), transcendentals=0
    )


def sds(shape, dtype):
    return jax.ShapeDtypeStruct(shape, dtype)


def relative_buckets():
    place = np.arange(2 * SPAN)
    relative = np.where(place < SPAN, -place, 2 * SPAN - place)
    distance = np.abs(relative)
    ratio = np.log(np.maximum(distance, 1) / 80.0) / math.log(10.0)
    beyond = np.minimum(80 + np.floor(ratio * 80.0).astype(np.int64), 159)
    bucket = np.where(relative > 0, 160, 0) + np.where(distance < 80, distance, beyond)
    return bucket.astype(np.int32)


SMEM = pl.BlockSpec(memory_space=pltpu.SMEM)
VMEM = pl.BlockSpec(memory_space=pltpu.VMEM)
ANY = pl.BlockSpec(memory_space=pl.ANY)


def call(kernel, name, us, out_shape, args, kinds, scratch=(), after=(), out_kinds=None, large=None):
    count = len(args)
    spaces = dict(s=SMEM, v=VMEM, a=ANY, p=VMEM)
    args = [pinned(x) if kind == "p" else x for x, kind in zip(args, kinds)]

    def run(*refs):
        kernel(*refs[:count], *refs[count + len(after) :])

    extra = {}
    outs = jax.tree.leaves(out_shape)
    if out_kinds:
        extra["out_specs"] = [spaces[k] for k in out_kinds]
    else:
        out_kinds = "v" * len(outs)
    held = [x for x, kind in zip([*args, *outs], kinds + out_kinds) if kind == "v"]
    held += [x for x in scratch if hasattr(x, "shape") and hasattr(x, "dtype")]
    held = [x for x in held if "sem" not in str(x.dtype)]
    return pl.pallas_call(
        run,
        in_specs=[spaces[k] for k in kinds] + [ANY] * len(after),
        out_shape=out_shape,
        scratch_shapes=list(scratch),
        compiler_params=params(large or sum(map(size_of, held)) >> 20),
        name=name,
        cost_estimate=cost(us),
        **extra,
    )(*args, *after)


def pinned(x):
    return pltpu.with_memory_space_constraint(x, pltpu.VMEM)


def hold(x, after, pin=False):
    def nothing(*refs):
        pass

    space = VMEM if pin else ANY
    return pl.pallas_call(
        nothing,
        in_specs=[space] + [ANY] * len(after),
        out_specs=space,
        out_shape=sds(x.shape, x.dtype),
        input_output_aliases={0: 0},
        name="hold",
        cost_estimate=cost(0.1),
    )(pinned(x) if pin else x, *after)


def lanes_of(shape):
    return lax.broadcasted_iota(jnp.int32, shape, len(shape) - 1)


def lines_of(shape):
    return lax.broadcasted_iota(jnp.int32, shape, len(shape) - 2)


def chosen_rows(order, visible, c, rows):
    slots = order[:, :rows]
    slots = jnp.sum(jnp.where(lines_of(slots.shape) == c, slots, 0), 0, keepdims=True)
    return jnp.where(lanes_of((1, rows)) < visible[c], slots, -1)


def one_hot(order, visible, c, rows, patches):
    slots = chosen_rows(order, visible, c, rows)
    return jnp.where(lines_of((patches, rows)) == slots, 1.0, 0.0).astype(BF16)


def widen(block, width):
    lines, lanes = block.shape
    return jnp.concatenate([block, jnp.zeros((lines, width - lanes), block.dtype)], 1)


def small_block(lines, table, width):
    heads = table.shape[0]
    table = jnp.concatenate([widen(table, 128), jnp.zeros((16 - heads, 128), F32)], 0)
    block = jnp.concatenate([lines, table], 1)
    return widen(block, width) if width > 256 else block


def first_kernel(where, query, key, value, out, *refs):
    vectors, up_b, table = refs[:8], refs[8], refs[9]
    own, quarter = refs[10:]
    share, width = query.shape
    for j, weight in enumerate((query, key, value, out)):
        own[j] = weight[...]
    quarter[:share, :] = own[where[0]]
    lines = [widen(v[...].astype(F32), 128) for v in vectors]
    for j in range(4):
        lines.append(widen(up_b[...].astype(F32)[:, j * share : (j + 1) * share], 128))
    lines.append(jnp.zeros((4, 128), F32))
    small = small_block(jnp.concatenate(lines, 0), table[...].astype(F32), width)
    quarter[share:, :] = small.astype(BF16)


def first_blocks(where, weights, vectors, up_b, table):
    share, width = weights[0].shape
    return call(
        first_kernel,
        "first_blocks",
        3,
        [sds((4, share, width), BF16), sds((share + 16, width), BF16)],
        [where, *weights, *vectors, up_b, table],
        "s" + "v" * 14,
        large=56,
    )


def up_blocks_kernel(where, up, own, quarter):
    width = quarter.shape[1]
    for j in range(4):
        own[j] = up[:, j * width : (j + 1) * width]
    quarter[...] = own[where[0]]


def up_blocks(where, up, width, after=()):
    share = up.shape[0]
    return call(
        up_blocks_kernel,
        "up_blocks",
        2,
        [sds((4, share, width), BF16), sds((share, width), BF16)],
        [where, up],
        "sv",
        after=after,
    )


def first_column_kernel(own, one, two, three, down, blocks, smalls, down_out, sem):
    share = blocks.shape[2]
    copy = pltpu.make_async_copy(down, down_out, sem)
    copy.start()
    for k, quarter in enumerate((own, one, two, three)):
        smalls[k] = quarter[share:, :]
        if k:
            for place in range(4):
                blocks[place, k - 1] = quarter[:share, :]
    copy.wait()


def first_column(own, arrived, down, after=()):
    share, width = own.shape[0] - 16, own.shape[1]
    return call(
        first_column_kernel,
        "first_column",
        2,
        [sds((4, 3, share, width), BF16), sds((4, 16, width), BF16), sds(down.shape, BF16)],
        [own, *arrived, down],
        "vvvva",
        [pltpu.SemaphoreType.DMA],
        after,
        "vva",
    )


def up_column_kernel(one, two, three, blocks):
    for k, quarter in enumerate((one, two, three)):
        for copy in range(4):
            blocks[copy, k] = quarter[...]


def up_column(arrived, after=()):
    return call(
        up_column_kernel,
        "up_column",
        2,
        sds((4, 3) + arrived[0].shape, BF16),
        arrived,
        "vvv",
        after=after,
    )


def gate_spread(gate_weight, width):
    half = gate_weight.shape[0] // 2
    size = gate_weight.shape[1]
    values = gate_weight[...]
    own = lanes_of((16, width)) // size == lines_of((16, width))
    spread = []
    for i in range(2):
        line = jnp.sum(values[i * half : (i + 1) * half], 0, keepdims=True)
        line = widen(line, 128)
        line = line + pltpu.roll(line, size, 1)
        line = jnp.concatenate([line] * (width // 128), 1)
        spread.append(jnp.where(own, line, 0.0))
    return jnp.concatenate(spread, 0)


def scale_lines(gate_scale, lanes):
    line = lines_of((16, lanes))
    scale = jnp.zeros((16, lanes), F32)
    for h in range(gate_scale.shape[0]):
        scale = jnp.where(line == h, gate_scale[h], scale)
    return scale


def pick_kernel(
    order, visible, gate_bias, gate_scale, tokens, gate_weight, token, picked, first, second, value,
    spread
):
    clip = pl.program_id(0)
    patches, width = tokens.shape[1:]
    rows = picked.shape[0]

    @pl.when(clip == 0)
    def _():
        spread[...] = gate_spread(gate_weight, width)

    chosen = dot(one_hot(order, visible, clip, rows, patches), tokens[0], TN)
    picked[...] = chosen.astype(BF16)
    logits = dot(spread[...], chosen, NT, HIGHEST)
    half = gate_bias.shape[0] // 2
    one = jax.nn.sigmoid(logits[:16] + sum(gate_bias[f] for f in range(half)))
    two = jax.nn.sigmoid(logits[16:] + sum(gate_bias[f + half] for f in range(half)))
    first[0] = one
    second[0] = two
    value[0] = one * (two * scale_lines(gate_scale, rows) - 1.0) + 2.0


def pick(order, visible, gate_bias, gate_scale, tokens, gate_weight, rows, after):
    clips, patches, width = tokens.shape
    whole = lambda *s: pl.BlockSpec(s, lambda c: (0,) * len(s))
    gate = pl.BlockSpec((1, 16, rows), lambda c: (c, 0, 0))
    return pl.pallas_call(
        pick_kernel,
        grid=(clips,),
        in_specs=[
            whole(*order.shape),
            SMEM,
            SMEM,
            SMEM,
            pl.BlockSpec((1, patches, width), lambda c: (c, 0, 0)),
            whole(*gate_weight.shape),
            ANY,
        ],
        out_specs=[pl.BlockSpec((rows, width), lambda c: (c, 0)), gate, gate, gate],
        out_shape=[sds((clips * rows, width), BF16)] + [sds((clips, 16, rows), F32)] * 3,
        scratch_shapes=[pltpu.VMEM((32, width), F32)],
        compiler_params=params(0, "arbitrary"),
        name="pick",
        cost_estimate=cost(6),
    )(order, visible, gate_bias, gate_scale, tokens, gate_weight, after)


def position_kernel(
    where, order, visible, buckets, *refs
):
    mine, other, out, vectors, held, levels, toeplitz, select = refs
    clips, pairs, rows = out.shape[:3]
    heads = 2 * pairs
    width = vectors.shape[1]
    share = width // 8
    held[0] = mine[...]
    held[1] = other[...]
    shards = [
        held[where[2] ^ (w % 2), where[1] ^ (w // 2)].astype(F32) for w in range(8)
    ]
    lane = lanes_of((16, 128))
    rows_of = [widen(jnp.where(lane < share, shard[:, :128], 0.0), width) for shard in shards]
    total = rows_of[0]
    for w in range(1, 8):
        total += pltpu.roll(rows_of[w], share * w, 1)
    vectors[0:8, :] = total[:8]
    chunk = []
    for k in range(4):
        line = jnp.zeros((1, width), F32)
        for half in range(2):
            for j in range(4):
                turn = 4 * share * half + share * j
                piece = rows_of[2 * k + half][8 + j : 9 + j]
                line += pltpu.roll(piece, turn, 1) if turn else piece
        chunk.append(line)
    vectors[8:16, :] = jnp.concatenate(chunk + [jnp.zeros((4, width), F32)], 0)
    count = NUM_BUCKETS // 8
    table = jnp.zeros((16, 384), F32)
    for w, shard in enumerate(shards):
        piece = widen(jnp.where(lane < count, shard[:, 128:256], 0.0), 384)
        table += pltpu.roll(piece, count * w, 1) if w else piece
    ids = lines_of((384, 2 * SPAN))
    onehot = jnp.where(ids == buckets[...], 1.0, 0.0).astype(BF16)
    levels[...] = dot(table.astype(BF16), onehot)
    for c in range(clips):
        select[:, c * rows : (c + 1) * rows] = one_hot(order, visible, c, rows, SPAN)

    def pair_step(pair, carry):
        for half in range(2):
            level = levels[pl.ds(2 * pair + half, 1), :]
            base = pltpu.roll(
                jnp.broadcast_to(level, (8, 2 * SPAN)), 0, 1, stride=1, stride_axis=0
            )
            for k in range(0, 16, 2):
                low = pltpu.roll(base, 8 * k, 1) if k else base
                block = jnp.concatenate([low, pltpu.roll(base, 8 * k + 8, 1)], 0).astype(BF16)
                for m in range(SPAN // 128):
                    for t in range(SPAN // 128):
                        source = ((t - m) % (SPAN // 64)) * 128
                        toeplitz[pl.ds(128 * m + 8 * k, 16), pl.ds(128 * t, 128)] = block[
                            :, source : source + 128
                        ]
            lines = dot(select[...], toeplitz[...], TN).astype(BF16)
            for c in range(clips):
                cut = slice(c * rows, (c + 1) * rows)
                out[c, pair, :, half * rows : (half + 1) * rows] = dot(
                    lines[cut], select[:, cut]
                ).astype(BF16)
        return carry

    lax.fori_loop(0, pairs, pair_step, 0)


def positions(where, order, visible, smalls, clips, rows, pairs, width):
    buckets = jnp.asarray(relative_buckets()[None, :])
    return call(
        position_kernel,
        "position",
        11,
        [sds((clips, pairs, rows, 2 * rows), BF16), sds((16, width), F32)],
        [where, order, visible, buckets, *smalls],
        "svsv" + "v" * 2,
        [
            pltpu.VMEM((2, 4, 16, width), BF16),
            pltpu.VMEM((16, 2 * SPAN), F32),
            pltpu.VMEM((SPAN, SPAN), BF16),
            pltpu.VMEM((SPAN, clips * rows), BF16),
        ],
        large=MOST,
    )


def two_heads(block):
    lane = lax.broadcasted_iota(jnp.int32, block.shape, 1)
    zero = jnp.zeros_like(block)
    half = block.shape[1] // 2
    return jnp.concatenate(
        [jnp.where(lane < half, block, zero), jnp.where(lane < half, zero, block)], 0
    )


def one_block(stacked):
    rows = stacked.shape[0] // 2
    lane = lax.broadcasted_iota(jnp.int32, (rows, stacked.shape[1]), 1)
    return jnp.where(lane < stacked.shape[1] // 2, stacked[:rows], stacked[rows:])


def unit_norm(values):
    center = values - jnp.mean(values, -1, keepdims=True)
    inverse = lax.rsqrt(jnp.mean(center * center, -1, keepdims=True) + EPS)
    return center * inverse, inverse


def load_squares(where, mine, other, weights, sem):
    share = weights.shape[1] // 8
    started = []

    def start(source, quarter, shard):
        line = pl.ds(pl.multiple_of(shard * share, share), share)
        copy = pltpu.make_async_copy(source, weights.at[quarter, line, :], sem)
        copy.start()
        started.append(copy)

    for side, (own, plane) in enumerate((mine, other)):
        core = where[2] ^ side
        for j in range(4):
            start(own.at[j], j, where[1] * 2 + core)
            for k in range(1, 4):
                start(plane.at[j, k - 1], j, (where[1] ^ k) * 2 + core)
    return started


def finish(copies):
    for copy in copies:
        copy.wait()


def attend_kernel(where, visible, picked, gates, position, vectors, *refs):
    mine, other = refs[:2], refs[2:4]
    query, key, value, soft, mixed, unit, inverse, normed, normed_low, weights, sem = refs[4:]
    clips, pairs, rows = position.shape[:3]
    finish(load_squares(where, mine, other, weights, sem))
    query_b, value_b, out_b = vectors[0:1, :], vectors[1:2, :], vectors[2:3, :]
    gain, shift = vectors[4:5, :], vectors[5:6, :]
    x = picked[...]
    query[...] = ((dot(x, weights[0]) + query_b).astype(BF16).astype(F32) * 0.125).astype(BF16)
    key[...] = dot(x, weights[1]).astype(BF16)
    value[...] = (dot(x, weights[2]) + value_b).astype(BF16)

    def clip_step(c, carry):
        cut = pl.ds(pl.multiple_of(c * rows, rows), rows)
        live = lines_of((rows, 2 * rows)) < visible[c]
        for pair in range(pairs):
            lanes = pl.ds(128 * pair, 128)
            scores = dot(key[cut, lanes], two_heads(query[cut, lanes]), NT)
            gate = jnp.concatenate(
                [gates[c, 2 * pair : 2 * pair + 1, :], gates[c, 2 * pair + 1 : 2 * pair + 2, :]], 1
            )
            scores = scores + gate * position[c, pair].astype(F32)
            scores = jnp.where(live, scores, -1000000000.0)
            exps = jnp.exp(scores - jnp.max(scores, 0, keepdims=True))
            exps = exps * (1.0 / jnp.sum(exps, 0, keepdims=True))
            low = exps.astype(BF16)
            soft[c, pair] = exps
            mixed[cut, lanes] = one_block(dot(low, value[cut, lanes], TN)).astype(BF16)
        return carry

    lax.fori_loop(0, clips, clip_step, 0)
    attended = dot(mixed[...], weights[3]) + out_b
    units, inv = unit_norm(ALPHA * x.astype(F32) + attended)
    unit[...] = units
    inverse[...] = inv
    result = units * gain + shift
    normed[...] = result
    normed_low[...] = result.astype(BF16)


def attend(where, visible, picked, gates, position, vectors, mine, other, after=()):
    clips, pairs, rows = position.shape[:3]
    total, width = picked.shape
    flat = sds((total, width), BF16)
    wide = sds((total, width), F32)
    return call(
        attend_kernel,
        "attend",
        14,
        [
            flat,
            flat,
            flat,
            sds((clips, pairs, rows, 2 * rows), F32),
            flat,
            wide,
            sds((total, 1), F32),
            wide,
            flat,
            sds((4, width, width), BF16),
        ],
        [where, visible, picked, gates, position, vectors, *mine, *other],
        "ssvvvv" + "a" * 4,
        [pltpu.SemaphoreType.DMA],
        after,
        large=MOST,
    )


def gelu_parts(x):
    size = jnp.abs(x) * (1.0 / math.sqrt(2.0))
    t = 1.0 / (1.0 + 0.3275911 * size)
    fall = jnp.exp(-0.5 * x * x)
    series = t * (
        0.5 * 0.254829592
        + t
        * (
            0.5 * -0.284496736
            + t * (0.5 * 1.421413741 + t * (0.5 * -1.453152027 + t * (0.5 * 1.061405429)))
        )
    )
    tail = series * fall
    below = jnp.where(x >= 0.0, 1.0 - tail, tail)
    return x * below, below + x * fall * (1.0 / math.sqrt(2.0 * math.pi))


def norm_back(grad, unit, inverse, gain):
    scaled = grad * gain
    return inverse * (
        scaled
        - jnp.mean(scaled, -1, keepdims=True)
        - unit * jnp.mean(scaled * unit, -1, keepdims=True)
    )


UPROWS = 256


def feed_kernel(where, visible, normed_low, normed, vectors, cotangent, *refs):
    ups, down = (refs[0:2], refs[2:4]), refs[4]
    down_keep, down_send, up_out, output, grad_normed, up_b_grad, sums = refs[5:12]
    (
        up_w, down_w, active, slope, branch, grad_branch, down_parts, up_parts, up_sem, down_sem,
        down_done, up_done,
    ) = refs[12:]
    chunks, rows, width = slope.shape
    share = width // 8
    clips = visible.shape[0]
    block = rows // clips
    depth, core = where[1], where[2]
    up_copies = load_squares(where, *ups, up_w, up_sem)
    down_copies = [pltpu.make_async_copy(down, down_w, down_sem)]
    down_copies[0].start()
    finish(up_copies)

    def up_step(k, carry):
        bias = vectors[pl.ds(8 + k, 1), :]
        parts = [
            dot(normed_low[r : r + UPROWS, :], up_w[k]) for r in range(0, rows, UPROWS)
        ]
        for i, part in enumerate(parts):
            activated, derivative = gelu_parts(part + bias)
            active[k, i * UPROWS : (i + 1) * UPROWS, :] = activated.astype(BF16)
            slope[k, i * UPROWS : (i + 1) * UPROWS, :] = derivative
        return carry

    lax.fori_loop(0, chunks, up_step, 0)
    finish(down_copies)
    total = dot(active[0], down_w[0])
    for k in range(1, chunks):
        total += dot(active[k], down_w[k])
    branch[...] = total
    gain, shift = vectors[6:7, :], vectors[7:8, :]
    sums[...] = jnp.zeros_like(sums)

    def norm_step(c, carry):
        cut = pl.ds(pl.multiple_of(c * block, block), block)
        units, inv = unit_norm(ALPHA * normed[cut, :] + branch[cut, :] + vectors[3:4, :])
        alive = jnp.where(lines_of((block, width)) < visible[c], 1.0, 0.0)
        output[cut, :] = ((units * gain + shift) * alive).astype(BF16)
        grad = cotangent[cut, :].astype(F32) * alive
        pre = norm_back(grad, units, inv, gain)
        grad_normed[cut, :] = ALPHA * pre
        low = pre.astype(BF16)
        grad_branch[cut, :] = low
        sums[0:1, :] += jnp.sum(grad * units, 0, keepdims=True)
        sums[1:2, :] += jnp.sum(grad, 0, keepdims=True)
        sums[2:3, :] += jnp.sum(low.astype(F32), 0, keepdims=True)
        return carry

    lax.fori_loop(0, clips, norm_step, 0)
    up_b_grad[...] = jnp.zeros_like(up_b_grad)
    down_out = lambda k: [
        pltpu.make_async_copy(down_parts.at[0, :, k], down_keep.at[:, k], down_done),
        pltpu.make_async_copy(down_parts.at[1, :, k], down_send.at[:, k], down_done),
    ]
    up_copy = lambda k: [
        pltpu.make_async_copy(
            up_parts.at[k], up_out.at[:, pl.ds(pl.multiple_of(k * width, width), width)], up_done
        )
    ]

    def down_step(k, carry):
        grad = dot(active[k], grad_branch[...], TN).astype(BF16)
        place = depth ^ k
        for side in range(2):
            for j in range(4):
                line = 4 * share * side + share * j
                down_parts[core ^ side, j, place] = grad[line : line + share]
        for copy in down_out(place):
            copy.start()
        return carry

    lax.fori_loop(0, chunks, down_step, 0)

    def up_back_step(k, carry):
        grad_hidden = dot(grad_branch[...], down_w[k], NT) * slope[k]
        grad_hidden = grad_hidden.astype(BF16)
        up_b_grad[pl.ds(k, 1), :] = jnp.sum(grad_hidden.astype(F32), 0, keepdims=True)
        up_parts[k] = dot(normed_low[...], grad_hidden, TN).astype(BF16)
        for copy in up_copy(k):
            copy.start()
        grad_normed[...] += dot(grad_hidden, up_w[k], NT)
        return carry

    lax.fori_loop(0, chunks, up_back_step, 0)
    for k in range(4):
        finish(down_out(k))
        finish(up_copy(k))


def feed(where, visible, normed_low, normed, vectors, cotangent, ups, down, after=()):
    rows, width = normed.shape
    chunks = 4
    part = sds((4, 4, width // 8, width), BF16)
    deep = pltpu.VMEM((chunks, width, width), BF16)
    long = pltpu.VMEM((chunks, rows, width), BF16)
    parts = pltpu.VMEM((2,) + part.shape, BF16)
    args = [where, visible, normed_low, normed, vectors, cotangent, *ups[0], *ups[1], down]
    return call(
        feed_kernel,
        "feed",
        32,
        [
            part,
            part,
            sds((width, chunks * width), BF16),
            sds((rows, width), BF16),
            sds((rows, width), F32),
            sds((8, width), F32),
            sds((8, width), F32),
        ],
        args,
        "ssvvvv" + "a" * 5,
        [
            deep,
            deep,
            long,
            pltpu.VMEM((chunks, rows, width), F32),
            pltpu.VMEM((rows, width), F32),
            pltpu.VMEM((rows, width), BF16),
            parts,
            deep,
        ]
        + [pltpu.SemaphoreType.DMA] * 4,
        after,
        "aaavvvv",
        large=MOST,
    )


def place_square(where, j, block, keep, send):
    share = block.shape[0] // 8
    core = where[2]
    for z in range(4):
        for side, target in ((core, keep), (1 - core, send)):
            line = pl.multiple_of(share * (2 * z + side), share)
            target[j, where[1] ^ z] = block[pl.ds(line, share), :]


def mix_back_kernel(
    grad_normed, unit, inverse, vectors, mixed, weights, grad_pre, out_grad, grad_mixed, sums
):
    width = grad_normed.shape[1]
    grad = grad_normed[...]
    units = unit[...]
    pre = norm_back(grad, units, inverse[...], vectors[4:5, :])
    grad_pre[...] = ALPHA * pre
    low = pre.astype(BF16)
    sums[0:1, :] = jnp.sum(grad * units, 0, keepdims=True)
    sums[1:2, :] = jnp.sum(grad, 0, keepdims=True)
    sums[2:3, :] = jnp.sum(low.astype(F32), 0, keepdims=True)
    sums[3:8, :] = jnp.zeros((5, width), F32)
    out_grad[...] = dot(mixed[...], low, TN).astype(BF16)
    grad_mixed[...] = dot(low, weights[0], NT).astype(BF16)


def mix_back(grad_normed, unit, inverse, vectors, mixed, weights, after=()):
    total, width = grad_normed.shape

    def run(*refs):
        mix_back_kernel(*refs[:6], *refs[6 + len(after) :])

    whole = lambda x: pl.BlockSpec(x.shape, lambda i: (0,) * len(x.shape))
    outs = [
        sds((total, width), F32),
        sds((width, width), BF16),
        sds((total, width), BF16),
        sds((8, width), F32),
    ]
    return pl.pallas_call(
        run,
        grid=(1,),
        in_specs=[whole(x) for x in (grad_normed, unit, inverse, vectors, mixed)]
        + [pl.BlockSpec((1, width, width), lambda i: (3, 0, 0))]
        + [ANY] * len(after),
        out_specs=[whole(x) for x in outs],
        out_shape=outs,
        compiler_params=params(),
        name="mix_back",
        cost_estimate=cost(6),
    )(grad_normed, unit, inverse, vectors, mixed, weights, *after)


def attend_back_kernel(
    where, grad_mixed, out_grad, picked, query, key, value, soft, position, gates, *refs
):
    keep, send, grad_query, grad_key, grad_value, grad_gate, gated_scores, sums = refs[-12:-4]
    queries, keys, values, block = refs[-4:]
    pairs, rows = position.shape[1:3]
    width = picked.shape[1]
    clip = pl.program_id(0)
    cut = pl.ds(pl.multiple_of(clip * rows, rows), rows)
    for pair in range(pairs):
        lanes = pl.ds(128 * pair, 128)
        weights = soft[0, pair]
        weights_low = weights.astype(BF16)
        back = two_heads(grad_mixed[:, lanes])
        grad_soft = dot(value[:, lanes], back, NT)
        grad_value[:, lanes] = dot(weights_low, back).astype(BF16)
        carried = jnp.sum(grad_soft * weights, 0, keepdims=True)
        low_scores = (weights * (grad_soft - carried)).astype(BF16)
        scores = low_scores.astype(F32)
        grad_key[:, lanes] = dot(low_scores, two_heads(query[:, lanes])).astype(BF16)
        grad_query[:, lanes] = (one_block(dot(low_scores, key[:, lanes], TN)) * 0.125).astype(BF16)
        gate = jnp.concatenate(
            [gates[0, 2 * pair : 2 * pair + 1, :], gates[0, 2 * pair + 1 : 2 * pair + 2, :]], 1
        )
        by_gate = jnp.sum(scores * position[0, pair].astype(F32), 0, keepdims=True)
        grad_gate[0, 2 * pair : 2 * pair + 1, :] = by_gate[:, :rows]
        grad_gate[0, 2 * pair + 1 : 2 * pair + 2, :] = by_gate[:, rows:]
        gated_scores[0, pair] = (scores * gate).astype(BF16)
    grad_gate[0, 2 * pairs :, :] = jnp.zeros((16 - 2 * pairs, rows), F32)
    queries[cut, :] = grad_query[...]
    keys[cut, :] = grad_key[...]
    values[cut, :] = grad_value[...]

    @pl.when(clip == pl.num_programs(0) - 1)
    def _():
        sums[0:1, :] = jnp.sum(queries[...].astype(F32), 0, keepdims=True)
        sums[1:2, :] = jnp.sum(values[...].astype(F32), 0, keepdims=True)
        sums[2:8, :] = jnp.zeros((6, width), F32)
        x = picked[...]
        for j, grad in enumerate((queries, keys, values)):
            block[...] = dot(x, grad[...], TN).astype(BF16)
            place_square(where, j, block, keep, send)
        place_square(where, 3, out_grad, keep, send)


def attend_back(
    where, grad_mixed, out_grad, picked, query, key, value, soft, position, gates, after=()
):
    clips, pairs, rows = position.shape[:3]
    total, width = picked.shape
    flat = sds((total, width), BF16)
    part = sds((4, 4, width // 8, width), BF16)
    whole = lambda *s: pl.BlockSpec(s, lambda c: (0,) * len(s))
    lines = pl.BlockSpec((rows, width), lambda c: (c, 0))
    square = pl.BlockSpec((1, pairs, rows, 2 * rows), lambda c: (c, 0, 0, 0))
    gate = pl.BlockSpec((1, 16, rows), lambda c: (c, 0, 0))
    return pl.pallas_call(
        attend_back_kernel,
        grid=(clips,),
        in_specs=[
            SMEM,
            lines,
            whole(width, width),
            whole(total, width),
            lines,
            lines,
            lines,
            square,
            square,
            gate,
        ]
        + [ANY] * len(after),
        out_specs=[
            whole(*part.shape),
            whole(*part.shape),
            lines,
            lines,
            lines,
            gate,
            square,
            whole(8, width),
        ],
        out_shape=[
            part,
            part,
            flat,
            flat,
            flat,
            sds((clips, 16, rows), F32),
            sds(position.shape, BF16),
            sds((8, width), F32),
        ],
        scratch_shapes=[pltpu.VMEM((total, width), BF16)] * 3
        + [pltpu.VMEM((width, width), BF16)],
        compiler_params=params(0, "arbitrary"),
        name="attend_back",
        cost_estimate=cost(15),
    )(
        where, grad_mixed, out_grad, picked, query, key, value, soft, position, gates, *after
    )


def table_kernel(order, visible, gated, out, select, picks):
    clips, pairs, rows = gated.shape[:3]
    heads, total = 2 * pairs, clips * rows
    for c in range(clips):
        select[:, c * rows : (c + 1) * rows] = one_hot(order, visible, c, rows, SPAN)
    out[...] = jnp.zeros_like(out)

    def pair_step(pair, carry):
        for half in range(2):
            for c in range(clips):
                cut = slice(c * rows, (c + 1) * rows)
                block = gated[c, pair, :, half * rows : (half + 1) * rows]
                picks[cut, :] = dot(block, select[:, cut], NT).astype(BF16)
            sums = dot(select[...], picks[...])
            base = None
            for k in range(16):
                parts = []
                for t in range(SPAN // 64):
                    part = None
                    for m in range(SPAN // 128):
                        column = (t + m) % (SPAN // 64)
                        if column < SPAN // 128:
                            line = 128 * m + 8 * k
                            block = sums[line : line + 8, 128 * column : 128 * column + 128]
                            part = block if part is None else part + block
                    parts.append(jnp.zeros((8, 128), F32) if part is None else part)
                line = jnp.concatenate(parts, 1)
                line = pltpu.roll(line, 2 * SPAN - 8 * k, 1) if k else line
                base = line if base is None else base + line
            level = base[0:1, :]
            for r in range(1, 8):
                level = level + pltpu.roll(base[r : r + 1, :], 2 * SPAN - r, 1)
            out[pl.ds(2 * pair + half, 1), :] = level
        return carry

    lax.fori_loop(0, pairs, pair_step, 0)


def table_levels(order, visible, gated, after=()):
    total = gated.shape[0] * gated.shape[2]
    return call(
        table_kernel,
        "table_back",
        12,
        sds((16, 2 * SPAN), F32),
        [order, visible, gated],
        "vsv",
        [pltpu.VMEM((SPAN, total), BF16), pltpu.VMEM((total, SPAN), BF16)],
        after,
        large=MOST,
    )


def tokens_kernel(
    order, visible, gate_scale, grad_pre, grad_query, grad_key, grad_value, weights, picked, first,
    second, grad_gate, gate_weight, tokens_grad, gate_sums, gate_mix, grad_picked
):
    clips, patches = tokens_grad.shape[:2]
    total, width = picked.shape
    rows = total // clips
    spread = gate_spread(gate_weight, width)
    scale = scale_lines(gate_scale, rows)
    logits = []
    by_scale = jnp.zeros((16, rows), F32)
    for c in range(clips):
        one, two, grad = first[c], second[c], grad_gate[c]
        by_scale += grad * one * two
        logits.append(
            jnp.concatenate(
                [
                    grad * (two * scale - 1.0) * one * (1.0 - one),
                    grad * one * scale * two * (1.0 - two),
                ],
                0,
            )
        )
    logits = jnp.concatenate(logits, 1)
    gate_sums[...] = jnp.zeros_like(gate_sums)
    gate_sums[0:8, 0:32] = dot(jnp.ones((8, total), F32), logits, NT, HIGHEST)
    gate_sums[0:8, 32:48] = dot(jnp.ones((8, rows), F32), by_scale, NT, HIGHEST)
    gate_mix[...] = dot(logits, picked[...].astype(F32), NN, HIGHEST)
    grad = (
        grad_pre[...]
        + dot(grad_query[...], weights[0], NT)
        + dot(grad_key[...], weights[1], NT)
        + dot(grad_value[...], weights[2], NT)
        + dot(logits, spread, TN, HIGHEST)
    )
    grad_picked[...] = grad.astype(BF16)
    for c in range(clips):
        tokens_grad[c] = dot(
            one_hot(order, visible, c, rows, patches), grad_picked[c * rows : (c + 1) * rows, :]
        ).astype(BF16)


def tokens_back(patches, args, after=()):
    order, visible, picked = args[0], args[1], args[8]
    clips = visible.shape[0]
    total, width = picked.shape
    return call(
        tokens_kernel,
        "tokens_back",
        11,
        [
            sds((clips, patches, width), BF16),
            sds((8, 128), F32),
            sds((32, width), F32),
        ],
        args,
        "vss" + "v" * 10,
        [pltpu.VMEM((total, width), BF16)],
        after,
        large=MOST,
    )


def small_grads_kernel(
    where, sums_feed, up_b_grad, sums_mix, sums_attend, levels, buckets, gate_sums, gate_mix,
    keep, send, blocks
):
    width = sums_feed.shape[1]
    share = width // 8
    vectors = jnp.concatenate(
        [
            sums_attend[0:2, :],
            sums_mix[2:3, :],
            sums_feed[2:3, :],
            sums_mix[0:2, :],
            sums_feed[0:2, :],
        ],
        0,
    )
    ids = lines_of((384, 2 * SPAN))
    onehot = jnp.where(ids == buckets[...], 1.0, 0.0)
    table = dot(levels[...], onehot, NT, HIGHEST)
    count = NUM_BUCKETS // 8
    mix = gate_mix[...]
    own = lanes_of((16, width)) // 64 == lines_of((16, width))
    gates = []
    for half in range(2):
        line = jnp.sum(jnp.where(own, mix[16 * half : 16 * half + 16], 0.0), 0, keepdims=True)
        total = line[:, 0:128]
        for t in range(1, width // 128):
            total += line[:, 128 * t : 128 * t + 128]
        total += pltpu.roll(total, 64, 1)
        gates.append(total)
    gates.append(gate_sums[0:1, :])
    gates.append(jnp.zeros((1, 128), F32))
    gates = jnp.concatenate(gates, 0)
    for w in range(8):
        turned = pltpu.roll(vectors, width - share * w, 1) if w else vectors
        chunk = up_b_grad[w // 2 : w // 2 + 1, :]
        lines = [turned[:, :128]]
        for j in range(4):
            turn = 4 * share * (w % 2) + share * j
            lines.append((pltpu.roll(chunk, width - turn, 1) if turn else chunk)[:, :128])
        lines.append(gates)
        turned = pltpu.roll(table, 384 - count * w, 1) if w else table
        blocks[w] = jnp.concatenate([jnp.concatenate(lines, 0), turned[:, :128]], 1)
    for z in range(4):
        keep[where[1] ^ z] = blocks[2 * z + where[2]]
        send[where[1] ^ z] = blocks[2 * z + 1 - where[2]]


def small_grads(where, sums_feed, up_b_grad, sums_mix, sums_attend, levels, gate_sums, gate_mix):
    buckets = jnp.asarray(relative_buckets()[None, :])
    part = sds((4, 16, 256), F32)
    return call(
        small_grads_kernel,
        "small_grads",
        4,
        [part, part],
        [where, sums_feed, up_b_grad, sums_mix, sums_attend, levels, buckets, gate_sums, gate_mix],
        "s" + "v" * 8,
        [pltpu.VMEM((8, 16, 256), F32)],
    )


def swap_wide(x, flip):
    size = lax.axis_size("wide")
    return lax.ppermute(x, "wide", [(i, i ^ flip) for i in range(size)])


def swap_narrow(x, flip):
    size = lax.axis_size("narrow")
    return lax.ppermute(x, "narrow", [(i, i ^ flip) for i in range(size)])


def column_of(quarter):
    return [swap_wide(quarter, 2 * k) for k in range(1, 4)]


def trade(parts):
    return lax.all_to_all(parts, "narrow", 0, 0)


def both_cores(own, plane):
    return (own, plane), (swap_wide(own, 1), swap_wide(plane, 1))


def core_sum_kernel(keep, came, *refs):
    refs[-1][...] = (keep[...].astype(F32) + came[...].astype(F32)).astype(BF16)


def core_sum(keep, came, after=()):
    return call(
        core_sum_kernel, "core_sum", 4, sds(keep.shape, BF16), [keep, came], "vv", after=after
    )


def sum_four(a, b, c, d):
    return (a.astype(F32) + b.astype(F32)) + (c.astype(F32) + d.astype(F32))


def plane_sum_kernel(parts, *refs):
    smalls, outs = refs[:-4], refs[-4:]
    share = parts.shape[2]
    for k, out in enumerate(outs):
        out[:share, :] = sum_four(*(parts[j, k] for j in range(4))).astype(BF16)
        if smalls:
            small = sum_four(*(small[k] for small in smalls))
            high = small.astype(BF16).astype(F32)
            split = jnp.concatenate([high, small - high], 1)
            out[share:, :] = widen(split, out.shape[1]).astype(BF16)


def plane_sum(parts, smalls=(), after=()):
    share, width = parts.shape[2:]
    share += sum(s.shape[1] for s in smalls[:1])
    out = [sds((share, width), BF16)] * 4
    args = [parts, *smalls]
    return call(plane_sum_kernel, "plane_sum", 30, out, args, "v" * len(args), after=after)


def up_parts_kernel(up, out):
    width = out.shape[2]
    for j in range(4):
        out[j] = up[:, j * width : (j + 1) * width]


def up_parts(up, width, after=()):
    share = up.shape[0]
    return call(
        up_parts_kernel, "up_parts", 0.01, sds((4, share, width), BF16), [up], "v", after=after
    )


def column_sum_kernel(a, b, c, d, out):
    total = sum_four(a[...], b[...], c[...], d[...]).astype(BF16)
    for j in range(4):
        out[j] = total


def column_sum(parts, after=()):
    out = sds((4,) + parts[0].shape, BF16)
    return call(column_sum_kernel, "column_sum", 20, out, parts, "vvvv", after=after)


def square_sum_kernel(a, b, c, d, out, small):
    share = out.shape[0]
    total = sum_four(a[...], b[...], c[...], d[...])
    out[...] = total[:share].astype(BF16)
    lanes = small.shape[1]
    small[...] = total[share:, :lanes] + total[share:, lanes : 2 * lanes]


def square_sum(parts, share, after=()):
    lines, width = parts[0].shape
    out = [sds((share, width), BF16), sds((lines - share, 256), F32)]
    return call(square_sum_kernel, "square_sum", 20, out, parts, "vvvv", after=after)


def end_sum_kernel(ups, square, out):
    up = sum_four(*(ups[j] for j in range(4))).astype(BF16)
    for j in range(4):
        out[j, 0] = up
        out[j, 1] = square[...]


def end_sum(ups, square, after=()):
    out = sds((4, 2) + square.shape, BF16)
    return call(end_sum_kernel, "end_sum", 2, out, [ups, square], "vv", after=after)


def last_kernel(*refs):
    ends, small, downs = refs[:3]
    query, key, value, out, up, down = refs[3:9]
    vectors = refs[9:18]
    table, gate_weight, gate_bias, gate_scale = refs[18:]
    share, width = query.shape
    for j, target in enumerate((query, key, value, out)):
        up[:, j * width : (j + 1) * width] = ends[j, 0].astype(F32)
        target[...] = ends[j, 1].astype(F32)
        down[j * share : (j + 1) * share, :] = downs[j].astype(F32)
    sums = small[:, :128]
    heads, count = table.shape
    table[...] = small[:heads, 128 : 128 + count]
    lines = [sums[i : i + 1, :share] for i in range(8)]
    up_b = jnp.concatenate(
        [sums[8 + j : 9 + j, :share] for j in range(4)], 1
    )
    query_b, value_b, out_b, down_b, gain1, shift1, gain2, shift2 = lines
    for target, line in zip(
        vectors, (query_b, value_b, out_b, up_b, down_b, gain1, shift1, gain2, shift2)
    ):
        target[...] = line
    logits, size = gate_weight.shape
    half = logits // 2
    gate_weight[...] = jnp.where(
        lines_of((logits, 128)) < half, sums[12:13, :], sums[13:14, :]
    )[:, :size]
    line = sums[14:15, :]
    at = lanes_of((1, 128))
    one = jnp.sum(jnp.where(at < 16, line, 0.0), 1, keepdims=True)
    two = jnp.sum(jnp.where((at >= 16) & (at < 32), line, 0.0), 1, keepdims=True)
    gate_bias[...] = jnp.where(at < half, one, two)[:, : 2 * half]
    gate_scale[...] = pltpu.roll(line, 96, 1)[:, :heads]


def last(ends, small, downs, heads, logits):
    share, width = ends.shape[2:]
    line = sds((1, share), F32)
    return call(
        last_kernel,
        "last",
        5,
        [sds((share, width), F32)] * 4
        + [sds((share, 4 * width), F32), sds((4 * share, width), F32)]
        + [line] * 3
        + [sds((1, 4 * share), F32)]
        + [line] * 5
        + [
            sds((heads, NUM_BUCKETS // 8), F32),
            sds((logits, width // heads), F32),
            sds((1, logits), F32),
            sds((1, heads), F32),
        ],
        [ends, small, downs],
        "vvv",
    )


def body(
    tokens,
    patch_order,
    visible,
    query_weight,
    key_weight,
    value_weight,
    out_weight,
    up_weight,
    down_weight,
    query_bias,
    value_bias,
    out_bias,
    up_bias,
    down_bias,
    first_gain,
    first_shift,
    second_gain,
    second_shift,
    bias_table,
    gate_weight,
    gate_bias,
    gate_scale,
    cotangent,
):
    clips, patches, width = tokens.shape
    rows = cotangent.shape[1]
    heads = bias_table.shape[1]
    pairs = heads // 2
    total = clips * rows
    hidden = up_weight.shape[1]
    share = width // 8
    n_wide, n_narrow = lax.axis_size("wide"), lax.axis_size("narrow")
    fast = n_wide == 8 and n_narrow == 4
    me_wide, me_narrow = lax.axis_index("wide"), lax.axis_index("narrow")
    vectors = [
        query_bias, value_bias, out_bias, down_bias,
        first_gain, first_shift, second_gain, second_shift,
    ]
    squares = [query_weight, key_weight, value_weight, out_weight]
    gate_lines = gate_weight.T
    gather = lambda x: lax.all_gather(x, "wide", axis=0, tiled=True)

    if fast:
        where = jnp.stack([me_narrow, me_wide // 2, me_wide % 2]).astype(jnp.int32)
        own_square, square_quarter = first_blocks(
            where, squares, [v[None, :] for v in vectors], up_bias[None, :], bias_table.T
        )
        picked, first, second, gates = pick(
            patch_order, visible, gate_bias, gate_scale, tokens, gate_lines, rows, square_quarter
        )
        own_up, up_quarter = up_blocks(where, up_weight, width, (picked,))
        column, small, down_copy = first_column(
            square_quarter, column_of(square_quarter), down_weight, (own_up,)
        )
        down_w = gather(down_copy)
        smalls = (small, swap_wide(small, 1))
        up_arrived = column_of(up_quarter)
        square_plane = trade(column)
    else:
        where = jnp.zeros((3,), jnp.int32)
        picked, first, second, gates = pick(
            patch_order, visible, gate_bias, gate_scale, tokens, gate_lines, rows, tokens
        )
        fold = lambda x: x.reshape(4, 2, share, width).transpose(1, 0, 2, 3)
        pack = lambda x: [(c[0], jnp.swapaxes(c[1:], 0, 1)) for c in (x[0], x[1])]
        square_blocks = pack(jnp.stack([fold(gather(w)) for w in squares], 2))
        ups = jnp.split(gather(up_weight), 4, 1)
        up_pieces = pack(jnp.stack([fold(u) for u in ups], 2))
        down_w = gather(down_weight)
        lines = [gather(v).reshape(8, 1, share) for v in vectors]
        lines += [gather(up_bias).reshape(8, 4, share), jnp.zeros((8, 4, share), BF16)]
        lines = jnp.pad(jnp.concatenate(lines, 1), ((0, 0), (0, 0), (0, 128 - share)))
        table = gather(bias_table).reshape(8, -1, heads).transpose(0, 2, 1)
        table = jnp.pad(table, ((0, 0), (0, 16 - heads), (0, 128 - table.shape[2])))
        small = jnp.concatenate([lines, table], 2)
        small = jnp.pad(small, ((0, 0), (0, 0), (0, width - 256))).reshape(4, 2, 16, width)
        smalls = (small[:, 0], small[:, 1])

    position, lines = positions(
        where, patch_order, visible, smalls, clips, rows, pairs, width
    )
    if fast:
        square_plane = hold(square_plane, (lines,))
        square_blocks = both_cores(own_square, square_plane)
        column = up_column(up_arrived, (lines,))
        up_plane = trade(hold(column, (square_plane,)))
    query, key, value, soft, mixed, unit, inverse, normed, normed_low, weights = attend(
        where, visible, picked, gates, position, lines, *square_blocks
    )
    if fast:
        up_pieces = both_cores(own_up, hold(up_plane, (normed_low,)))
    down_keep, down_send, up_grad, output, grad_normed, up_b_grad, sums_feed = feed(
        where, visible, normed_low, normed, lines, cotangent.reshape(total, width),
        up_pieces, down_w.reshape(4, width, width),
    )
    grad_pre1, out_grad, grad_mixed, sums_mix = mix_back(
        grad_normed, unit, inverse, lines, mixed, weights
    )
    later = ()
    if fast:
        up_sum = lax.psum_scatter(up_grad, "wide", scatter_dimension=0, tiled=True)
        down_parts = core_sum(down_keep, swap_wide(down_send, 1), after=(grad_mixed,))
        later = (down_parts,)
    (
        square_keep, square_send, grad_query, grad_key, grad_value, grad_gate, gated, sums_attend,
    ) = attend_back(
        where, grad_mixed, out_grad, picked, query, key, value, soft, position, gates, later
    )
    levels = table_levels(patch_order, visible, gated)
    later = (levels,)
    if fast:
        square_parts = core_sum(square_keep, swap_wide(square_send, 1), after=(levels,))
        down_parts = plane_sum(trade(down_parts), after=(square_parts,))
        later = (down_parts[0],)
    tokens_grad, gate_sums, gate_mix = tokens_back(
        patches,
        [
            patch_order, visible, gate_scale, grad_pre1, grad_query, grad_key, grad_value, weights,
            picked, first, second, grad_gate, gate_lines,
        ],
        later,
    )
    small_keep, small_send = small_grads(
        where, sums_feed, up_b_grad, sums_mix, sums_attend, levels, gate_sums, gate_mix
    )

    if fast:
        spread = lambda parts: [parts[0]] + [swap_wide(parts[k], 2 * k) for k in range(1, 4)]
        up_part = up_parts(up_sum, width, (small_keep,))
        down_part = column_sum(spread(down_parts), (up_part,))
        small = small_keep + hold(swap_wide(small_send, 1), (down_part,))
        smalls = [small] + [swap_narrow(small, m) for m in range(1, 4)]
        square_plane = trade(square_parts)
        square_parts = plane_sum(square_plane, smalls)
        downs = trade(hold(down_part, (square_plane,)))
        ups = trade(hold(up_part, (downs,)))
        square, small = square_sum(spread(square_parts), share)
        ends = trade(end_sum(ups, square))
        ends = last(ends, small, downs, heads, gate_lines.shape[0])
        weight_grads, ends = ends[:6], ends[6:]
        vector_grads = [v.reshape(-1) for v in ends[:9]]
        table_grad, gate_weight_grad = ends[9].T, ends[10].T
        gate_bias_grad, gate_scale_grad = ends[11].reshape(-1), ends[12].reshape(-1)
    else:
        def reduce(x):
            x = lax.psum_scatter(x, "wide", scatter_dimension=0, tiled=True)
            return lax.psum(x, "narrow").astype(F32)

        def mine(x):
            part = x.shape[0] // n_wide
            return lax.dynamic_slice_in_dim(x, me_wide * part, part, 0)

        square = jnp.stack([square_keep, square_send], 2).reshape(4, width, width)
        down = jnp.stack([down_keep, down_send]).transpose(2, 0, 1, 3, 4).reshape(hidden, width)
        weight_grads = [reduce(square[j]) for j in range(4)]
        weight_grads += [reduce(up_grad), reduce(down)]
        small = jnp.stack([small_keep, small_send], 1).reshape(8, 16, 256)
        small = lax.psum(small, ("narrow", "wide"))
        lines = small[:, :8, :share].transpose(1, 0, 2).reshape(8, width)
        up_b_grad = small[:, 8:12, :share].reshape(-1)
        query_b, value_b, out_b, down_b, gain1, shift1, gain2, shift2 = lines
        vector_grads = [
            mine(v)
            for v in (query_b, value_b, out_b, up_b_grad, down_b, gain1, shift1, gain2, shift2)
        ]
        table = small[:, :heads, 128 : 128 + NUM_BUCKETS // 8].transpose(0, 2, 1)
        table_grad = mine(table.reshape(-1, heads))
        size, half = gate_weight.shape[0], gate_weight.shape[1] // 2
        gate_weight_grad = jnp.repeat(small[0, 12:14, :size].T, half, 1)
        gate_bias_grad = jnp.repeat(jnp.sum(small[0, 14, :32].reshape(2, 16), 1), half)
        gate_scale_grad = small[0, 14, 32 : 32 + heads]
    return (
        output.reshape(clips, rows, width),
        tokens_grad,
        *weight_grads,
        *vector_grads,
        table_grad,
        gate_weight_grad,
        gate_bias_grad,
        gate_scale_grad,
    )


def solution(mesh):
    split = P(("narrow", "wide"))
    shard = P("wide")
    in_specs = (split,) * 3 + (shard,) * 16 + (P(),) * 3 + (split,)
    out_specs = (split,) * 2 + (shard,) * 16 + (P(),) * 3
    return jax.shard_map(body, mesh=mesh, in_specs=in_specs, out_specs=out_specs, check_vma=False)
```

```python
from functools import partial
import math

import jax
import jax.numpy as jnp
import numpy as np
from jax import lax
from jax.experimental import pallas as pl
from jax.experimental.pallas import tpu as pltpu
from jax.sharding import PartitionSpec as P

NUM_BUCKETS = 320
SPAN = 512
SPARE = 4
MOST = 51
HIGHEST = lax.Precision.HIGHEST
ALPHA = math.pow(24.0, 0.25)
EPS = 1e-05
F32 = jnp.float32
BF16 = jnp.bfloat16
NN = (((1,), (0,)), ((), ()))
NT = (((1,), (1,)), ((), ()))
TN = (((0,), (0,)), ((), ()))


def dot(a, b, dims=NN, precision=None):
    return lax.dot_general(a, b, dims, precision=precision, preferred_element_type=F32)


def params(need=0, *semantics):
    extra = dict(dimension_semantics=semantics) if semantics else {}
    need = need if need > 50 else min(need + SPARE, MOST) if need else MOST
    return pltpu.CompilerParams(vmem_limit_bytes=need * 1024 * 1024, **extra)


def size_of(x):
    shape = list(x.shape)
    shape[-1] = -(-shape[-1] // 1024) * 1024 if len(shape) == 1 else -(-shape[-1] // 128) * 128
    if len(shape) > 1:
        shape[-2] = -(-shape[-2] // 8) * 8
    return math.prod(shape) * jnp.dtype(x.dtype).itemsize


def cost(us):
    return pl.CostEstimate(
        flops=int(us * 1e10), bytes_accessed=int(us * 3.5e7), transcendentals=0
    )


def sds(shape, dtype):
    return jax.ShapeDtypeStruct(shape, dtype)


def relative_buckets():
    place = np.arange(2 * SPAN)
    relative = np.where(place < SPAN, -place, 2 * SPAN - place)
    distance = np.abs(relative)
    ratio = np.log(np.maximum(distance, 1) / 80.0) / math.log(10.0)
    beyond = np.minimum(80 + np.floor(ratio * 80.0).astype(np.int64), 159)
    bucket = np.where(relative > 0, 160, 0) + np.where(distance < 80, distance, beyond)
    return bucket.astype(np.int32)


SMEM = pl.BlockSpec(memory_space=pltpu.SMEM)
VMEM = pl.BlockSpec(memory_space=pltpu.VMEM)
ANY = pl.BlockSpec(memory_space=pl.ANY)


def call(kernel, name, us, out_shape, args, kinds, scratch=(), after=(), out_kinds=None, large=None):
    count = len(args)
    spaces = dict(s=SMEM, v=VMEM, a=ANY, p=VMEM)
    args = [pinned(x) if kind == "p" else x for x, kind in zip(args, kinds)]

    def run(*refs):
        kernel(*refs[:count], *refs[count + len(after) :])

    extra = {}
    outs = jax.tree.leaves(out_shape)
    if out_kinds:
        extra["out_specs"] = [spaces[k] for k in out_kinds]
    else:
        out_kinds = "v" * len(outs)
    held = [x for x, kind in zip([*args, *outs], kinds + out_kinds) if kind == "v"]
    held += [x for x in scratch if hasattr(x, "shape") and hasattr(x, "dtype")]
    held = [x for x in held if "sem" not in str(x.dtype)]
    return pl.pallas_call(
        run,
        in_specs=[spaces[k] for k in kinds] + [ANY] * len(after),
        out_shape=out_shape,
        scratch_shapes=list(scratch),
        compiler_params=params(large or sum(map(size_of, held)) >> 20),
        name=name,
        cost_estimate=cost(us),
        **extra,
    )(*args, *after)


def pinned(x):
    return pltpu.with_memory_space_constraint(x, pltpu.VMEM)


def hold(x, after, pin=False):
    def nothing(*refs):
        pass

    space = VMEM if pin else ANY
    return pl.pallas_call(
        nothing,
        in_specs=[space] + [ANY] * len(after),
        out_specs=space,
        out_shape=sds(x.shape, x.dtype),
        input_output_aliases={0: 0},
        name="hold",
        cost_estimate=cost(0.1),
    )(pinned(x) if pin else x, *after)


def lanes_of(shape):
    return lax.broadcasted_iota(jnp.int32, shape, len(shape) - 1)


def lines_of(shape):
    return lax.broadcasted_iota(jnp.int32, shape, len(shape) - 2)


def chosen_rows(order, visible, c, rows):
    slots = order[:, :rows]
    slots = jnp.sum(jnp.where(lines_of(slots.shape) == c, slots, 0), 0, keepdims=True)
    return jnp.where(lanes_of((1, rows)) < visible[c], slots, -1)


def one_hot(order, visible, c, rows, patches):
    slots = chosen_rows(order, visible, c, rows)
    return jnp.where(lines_of((patches, rows)) == slots, 1.0, 0.0).astype(BF16)


def widen(block, width):
    lines, lanes = block.shape
    return jnp.concatenate([block, jnp.zeros((lines, width - lanes), block.dtype)], 1)


def small_block(lines, table, width):
    heads = table.shape[0]
    table = jnp.concatenate([widen(table, 128), jnp.zeros((16 - heads, 128), F32)], 0)
    block = jnp.concatenate([lines, table], 1)
    return widen(block, width) if width > 256 else block


def first_kernel(query, key, value, out, *refs):
    vectors, up_b, table = refs[:8], refs[8], refs[9]
    own, quarter = refs[10:]
    share, width = query.shape
    for j, weight in enumerate((query, key, value, out)):
        own[j] = weight[...]
    quarter[:share, :] = own[lax.axis_index("narrow")]
    lines = [widen(v[...].astype(F32), 128) for v in vectors]
    wide_b = up_b[...].astype(F32).reshape(1, 4 * share)
    for j in range(4):
        lines.append(widen(wide_b[:, j * share : (j + 1) * share], 128))
    lines.append(jnp.zeros((4, 128), F32))
    small = small_block(jnp.concatenate(lines, 0), table[...].astype(F32), width)
    quarter[share:, :] = small.astype(BF16)


def first_blocks(weights, vectors, up_b, table):
    share, width = weights[0].shape
    return call(
        first_kernel,
        "first_blocks",
        3,
        [sds((4, share, width), BF16), sds((share + 16, width), BF16)],
        [*weights, *vectors, up_b, table],
        "v" * 14,
        large=56,
    )


def up_blocks_kernel(where, up, own, quarter):
    width = quarter.shape[1]
    for j in range(4):
        own[j] = up[:, j * width : (j + 1) * width]
    quarter[...] = own[where[0]]


def up_blocks(where, up, width, after=()):
    share = up.shape[0]
    return call(
        up_blocks_kernel,
        "up_blocks",
        2,
        [sds((4, share, width), BF16), sds((share, width), BF16)],
        [where, up],
        "sv",
        after=after,
    )


def first_column_kernel(own, one, two, three, down, blocks, smalls, down_out, sem):
    share = blocks.shape[2]
    copy = pltpu.make_async_copy(down, down_out, sem)
    copy.start()
    for k, quarter in enumerate((own, one, two, three)):
        smalls[k] = quarter[share:, :]
        if k:
            for place in range(4):
                blocks[place, k - 1] = quarter[:share, :]
    copy.wait()


def first_column(own, arrived, down, after=()):
    share, width = own.shape[0] - 16, own.shape[1]
    return call(
        first_column_kernel,
        "first_column",
        2,
        [sds((4, 3, share, width), BF16), sds((4, 16, width), BF16), sds(down.shape, BF16)],
        [own, *arrived, down],
        "vvvva",
        [pltpu.SemaphoreType.DMA],
        after,
        "vva",
    )


def up_column_kernel(one, two, three, blocks):
    for k, quarter in enumerate((one, two, three)):
        for copy in range(4):
            blocks[copy, k] = quarter[...]


def up_column(arrived, after=()):
    return call(
        up_column_kernel,
        "up_column",
        2,
        sds((4, 3) + arrived[0].shape, BF16),
        arrived,
        "vvv",
        after=after,
    )


def gate_spread(gate_weight, width):
    half = gate_weight.shape[0] // 2
    size = gate_weight.shape[1]
    values = gate_weight[...]
    own = lanes_of((16, width)) // size == lines_of((16, width))
    spread = []
    for i in range(2):
        line = jnp.sum(values[i * half : (i + 1) * half], 0, keepdims=True)
        line = widen(line, 128)
        line = line + pltpu.roll(line, size, 1)
        line = jnp.concatenate([line] * (width // 128), 1)
        spread.append(jnp.where(own, line, 0.0))
    return jnp.concatenate(spread, 0)


def scale_lines(gate_scale, lanes):
    line = lines_of((16, lanes))
    scale = jnp.zeros((16, lanes), F32)
    for h in range(gate_scale.shape[0]):
        scale = jnp.where(line == h, gate_scale[h], scale)
    return scale


def pick_kernel(
    order, visible, gate_bias, gate_scale, tokens, gate_weight, token, picked, first, second, value,
    spread
):
    clip = pl.program_id(0)
    patches, width = tokens.shape[1:]
    rows = picked.shape[0]

    @pl.when(clip == 0)
    def _():
        spread[...] = gate_spread(gate_weight, width)

    chosen = dot(one_hot(order, visible, clip, rows, patches), tokens[0], TN)
    picked[...] = chosen.astype(BF16)
    logits = dot(spread[...], chosen, NT, HIGHEST)
    half = gate_bias.shape[0] // 2
    one = jax.nn.sigmoid(logits[:16] + sum(gate_bias[f] for f in range(half)))
    two = jax.nn.sigmoid(logits[16:] + sum(gate_bias[f + half] for f in range(half)))
    first[0] = one
    second[0] = two
    value[0] = one * (two * scale_lines(gate_scale, rows) - 1.0) + 2.0


def pick(order, visible, gate_bias, gate_scale, tokens, gate_weight, rows, after):
    clips, patches, width = tokens.shape
    whole = lambda *s: pl.BlockSpec(s, lambda c: (0,) * len(s))
    gate = pl.BlockSpec((1, 16, rows), lambda c: (c, 0, 0))
    return pl.pallas_call(
        pick_kernel,
        grid=(clips,),
        in_specs=[
            whole(*order.shape),
            SMEM,
            SMEM,
            SMEM,
            pl.BlockSpec((1, patches, width), lambda c: (c, 0, 0)),
            whole(*gate_weight.shape),
            ANY,
        ],
        out_specs=[pl.BlockSpec((rows, width), lambda c: (c, 0)), gate, gate, gate],
        out_shape=[sds((clips * rows, width), BF16)] + [sds((clips, 16, rows), F32)] * 3,
        scratch_shapes=[pltpu.VMEM((32, width), F32)],
        compiler_params=params(0, "arbitrary"),
        name="pick",
        cost_estimate=cost(6),
    )(order, visible, gate_bias, gate_scale, tokens, gate_weight, after)


def position_kernel(
    where, order, visible, buckets, *refs
):
    mine, other, out, vectors, held, levels, toeplitz, select = refs
    clips, pairs, rows = out.shape[:3]
    heads = 2 * pairs
    width = vectors.shape[1]
    share = width // 8
    held[0] = mine[...]
    held[1] = other[...]
    shards = [
        held[where[2] ^ (w % 2), where[1] ^ (w // 2)].astype(F32) for w in range(8)
    ]
    lane = lanes_of((16, 128))
    rows_of = [widen(jnp.where(lane < share, shard[:, :128], 0.0), width) for shard in shards]
    total = rows_of[0]
    for w in range(1, 8):
        total += pltpu.roll(rows_of[w], share * w, 1)
    vectors[0:8, :] = total[:8]
    chunk = []
    for k in range(4):
        line = jnp.zeros((1, width), F32)
        for half in range(2):
            for j in range(4):
                turn = 4 * share * half + share * j
                piece = rows_of[2 * k + half][8 + j : 9 + j]
                line += pltpu.roll(piece, turn, 1) if turn else piece
        chunk.append(line)
    vectors[8:16, :] = jnp.concatenate(chunk + [jnp.zeros((4, width), F32)], 0)
    count = NUM_BUCKETS // 8
    table = jnp.zeros((16, 384), F32)
    for w, shard in enumerate(shards):
        piece = widen(jnp.where(lane < count, shard[:, 128:256], 0.0), 384)
        table += pltpu.roll(piece, count * w, 1) if w else piece
    ids = lines_of((384, 2 * SPAN))
    onehot = jnp.where(ids == buckets[...], 1.0, 0.0).astype(BF16)
    levels[...] = dot(table.astype(BF16), onehot)
    for c in range(clips):
        select[:, c * rows : (c + 1) * rows] = one_hot(order, visible, c, rows, SPAN)

    def pair_step(pair, carry):
        for half in range(2):
            level = levels[pl.ds(2 * pair + half, 1), :]
            base = pltpu.roll(
                jnp.broadcast_to(level, (8, 2 * SPAN)), 0, 1, stride=1, stride_axis=0
            )
            for k in range(0, 16, 2):
                low = pltpu.roll(base, 8 * k, 1) if k else base
                block = jnp.concatenate([low, pltpu.roll(base, 8 * k + 8, 1)], 0).astype(BF16)
                for m in range(SPAN // 128):
                    for t in range(SPAN // 128):
                        source = ((t - m) % (SPAN // 64)) * 128
                        toeplitz[pl.ds(128 * m + 8 * k, 16), pl.ds(128 * t, 128)] = block[
                            :, source : source + 128
                        ]
            lines = dot(select[...], toeplitz[...], TN).astype(BF16)
            for c in range(clips):
                cut = slice(c * rows, (c + 1) * rows)
                out[c, pair, :, half * rows : (half + 1) * rows] = dot(
                    lines[cut], select[:, cut]
                ).astype(BF16)
        return carry

    lax.fori_loop(0, pairs, pair_step, 0)


def positions(where, order, visible, smalls, clips, rows, pairs, width):
    buckets = jnp.asarray(relative_buckets()[None, :])
    return call(
        position_kernel,
        "position",
        11,
        [sds((clips, pairs, rows, 2 * rows), BF16), sds((16, width), F32)],
        [where, order, visible, buckets, *smalls],
        "svsv" + "v" * 2,
        [
            pltpu.VMEM((2, 4, 16, width), BF16),
            pltpu.VMEM((16, 2 * SPAN), F32),
            pltpu.VMEM((SPAN, SPAN), BF16),
            pltpu.VMEM((SPAN, clips * rows), BF16),
        ],
        large=MOST,
    )


def two_heads(block):
    lane = lax.broadcasted_iota(jnp.int32, block.shape, 1)
    zero = jnp.zeros_like(block)
    half = block.shape[1] // 2
    return jnp.concatenate(
        [jnp.where(lane < half, block, zero), jnp.where(lane < half, zero, block)], 0
    )


def one_block(stacked):
    rows = stacked.shape[0] // 2
    lane = lax.broadcasted_iota(jnp.int32, (rows, stacked.shape[1]), 1)
    return jnp.where(lane < stacked.shape[1] // 2, stacked[:rows], stacked[rows:])


def unit_norm(values):
    center = values - jnp.mean(values, -1, keepdims=True)
    inverse = lax.rsqrt(jnp.mean(center * center, -1, keepdims=True) + EPS)
    return center * inverse, inverse


def load_squares(where, mine, other, weights, sems):
    share = weights.shape[1] // 8
    quarters = []
    for j in range(4):
        started = []
        for side, (own, plane) in enumerate((mine, other)):
            core = where[2] ^ side
            sources = [own.at[j]] + [plane.at[j, k - 1] for k in range(1, 4)]
            for k, source in enumerate(sources):
                shard = (where[1] ^ k) * 2 + core
                line = pl.ds(pl.multiple_of(shard * share, share), share)
                copy = pltpu.make_async_copy(source, weights.at[j, line, :], sems.at[j])
                copy.start()
                started.append(copy)
        quarters.append(started)
    return quarters


def finish(copies):
    for copy in copies:
        copy.wait()


def attend_kernel(where, visible, picked, gates, position, vectors, *refs):
    mine, other = refs[:2], refs[2:4]
    query, key, value, soft, mixed, unit, inverse, normed, normed_low, weights, sem = refs[4:]
    clips, pairs, rows = position.shape[:3]
    quarters = load_squares(where, mine, other, weights, sem)
    finish(quarters[0])
    query_b, value_b, out_b = vectors[0:1, :], vectors[1:2, :], vectors[2:3, :]
    gain, shift = vectors[4:5, :], vectors[5:6, :]
    x = picked[...]
    query[...] = ((dot(x, weights[0]) + query_b).astype(BF16).astype(F32) * 0.125).astype(BF16)
    finish(quarters[1])
    key[...] = dot(x, weights[1]).astype(BF16)
    finish(quarters[2])
    value[...] = (dot(x, weights[2]) + value_b).astype(BF16)

    def clip_step(c, carry):
        cut = pl.ds(pl.multiple_of(c * rows, rows), rows)
        live = lines_of((rows, 2 * rows)) < visible[c]
        for pair in range(pairs):
            lanes = pl.ds(128 * pair, 128)
            scores = dot(key[cut, lanes], two_heads(query[cut, lanes]), NT)
            gate = jnp.concatenate(
                [gates[c, 2 * pair : 2 * pair + 1, :], gates[c, 2 * pair + 1 : 2 * pair + 2, :]], 1
            )
            scores = scores + gate * position[c, pair].astype(F32)
            scores = jnp.where(live, scores, -1000000000.0)
            exps = jnp.exp(scores - jnp.max(scores, 0, keepdims=True))
            exps = exps * (1.0 / jnp.sum(exps, 0, keepdims=True))
            low = exps.astype(BF16)
            soft[c, pair] = exps
            mixed[cut, lanes] = one_block(dot(low, value[cut, lanes], TN)).astype(BF16)
        return carry

    lax.fori_loop(0, clips, clip_step, 0)
    finish(quarters[3])
    attended = dot(mixed[...], weights[3]) + out_b
    units, inv = unit_norm(ALPHA * x.astype(F32) + attended)
    unit[...] = units
    inverse[...] = inv
    result = units * gain + shift
    normed[...] = result
    normed_low[...] = result.astype(BF16)


def attend(where, visible, picked, gates, position, vectors, mine, other, after=()):
    clips, pairs, rows = position.shape[:3]
    total, width = picked.shape
    flat = sds((total, width), BF16)
    wide = sds((total, width), F32)
    return call(
        attend_kernel,
        "attend",
        14,
        [
            flat,
            flat,
            flat,
            sds((clips, pairs, rows, 2 * rows), F32),
            flat,
            wide,
            sds((total, 1), F32),
            wide,
            flat,
            sds((4, width, width), BF16),
        ],
        [where, visible, picked, gates, position, vectors, *mine, *other],
        "ssvvvv" + "a" * 4,
        [pltpu.SemaphoreType.DMA((4,))],
        after,
        large=MOST,
    )


def gelu_parts(x):
    size = jnp.abs(x) * (1.0 / math.sqrt(2.0))
    t = 1.0 / (1.0 + 0.3275911 * size)
    fall = jnp.exp(-0.5 * x * x)
    series = t * (
        0.5 * 0.254829592
        + t
        * (
            0.5 * -0.284496736
            + t * (0.5 * 1.421413741 + t * (0.5 * -1.453152027 + t * (0.5 * 1.061405429)))
        )
    )
    tail = series * fall
    below = jnp.where(x >= 0.0, 1.0 - tail, tail)
    return x * below, below + x * fall * (1.0 / math.sqrt(2.0 * math.pi))


def norm_back(grad, unit, inverse, gain):
    scaled = grad * gain
    return inverse * (
        scaled
        - jnp.mean(scaled, -1, keepdims=True)
        - unit * jnp.mean(scaled * unit, -1, keepdims=True)
    )


UPROWS = 256


def feed_kernel(where, visible, normed_low, normed, vectors, cotangent, *refs):
    ups, down = (refs[0:2], refs[2:4]), refs[4]
    down_keep, down_send, up_out, output, grad_normed, up_b_grad, sums = refs[5:12]
    (
        up_w, down_w, active, slope, branch, grad_branch, down_parts, up_parts, up_sem, down_sem,
        down_done, up_done,
    ) = refs[12:]
    chunks, rows, width = slope.shape
    share = width // 8
    clips = visible.shape[0]
    block = rows // clips
    depth, core = where[1], where[2]
    up_copies = load_squares(where, *ups, up_w, up_sem)
    down_copies = [pltpu.make_async_copy(down, down_w, down_sem)]
    down_copies[0].start()
    for k in range(chunks):
        finish(up_copies[k])
        for r in range(0, rows, UPROWS):
            cut = slice(r, r + UPROWS)
            hidden = dot(normed_low[cut, :], up_w[k]) + vectors[8 + k : 9 + k, :]
            activated, derivative = gelu_parts(hidden)
            active[k, cut, :] = activated.astype(BF16)
            slope[k, cut, :] = derivative
    finish(down_copies)
    total = dot(active[0], down_w[0])
    for k in range(1, chunks):
        total += dot(active[k], down_w[k])
    branch[...] = total
    gain, shift = vectors[6:7, :], vectors[7:8, :]
    sums[...] = jnp.zeros_like(sums)

    def norm_step(c, carry):
        cut = pl.ds(pl.multiple_of(c * block, block), block)
        units, inv = unit_norm(ALPHA * normed[cut, :] + branch[cut, :] + vectors[3:4, :])
        alive = jnp.where(lines_of((block, width)) < visible[c], 1.0, 0.0)
        output[cut, :] = ((units * gain + shift) * alive).astype(BF16)
        grad = cotangent[cut, :].astype(F32) * alive
        pre = norm_back(grad, units, inv, gain)
        grad_normed[cut, :] = ALPHA * pre
        low = pre.astype(BF16)
        grad_branch[cut, :] = low
        sums[0:1, :] += jnp.sum(grad * units, 0, keepdims=True)
        sums[1:2, :] += jnp.sum(grad, 0, keepdims=True)
        sums[2:3, :] += jnp.sum(low.astype(F32), 0, keepdims=True)
        return carry

    lax.fori_loop(0, clips, norm_step, 0)
    up_b_grad[...] = jnp.zeros_like(up_b_grad)
    down_out = lambda k: [
        pltpu.make_async_copy(down_parts.at[0, :, k], down_keep.at[:, k], down_done),
        pltpu.make_async_copy(down_parts.at[1, :, k], down_send.at[:, k], down_done),
    ]
    up_copy = lambda k: [
        pltpu.make_async_copy(
            up_parts.at[k], up_out.at[:, pl.ds(pl.multiple_of(k * width, width), width)], up_done
        )
    ]

    def down_step(k, carry):
        grad = dot(active[k], grad_branch[...], TN).astype(BF16)
        place = depth ^ k
        for side in range(2):
            for j in range(4):
                line = 4 * share * side + share * j
                down_parts[core ^ side, j, place] = grad[line : line + share]
        for copy in down_out(place):
            copy.start()
        return carry

    lax.fori_loop(0, chunks, down_step, 0)

    def up_back_step(k, carry):
        grad_hidden = dot(grad_branch[...], down_w[k], NT) * slope[k]
        grad_hidden = grad_hidden.astype(BF16)
        up_b_grad[pl.ds(k, 1), :] = jnp.sum(grad_hidden.astype(F32), 0, keepdims=True)
        up_parts[k] = dot(normed_low[...], grad_hidden, TN).astype(BF16)
        for copy in up_copy(k):
            copy.start()
        grad_normed[...] += dot(grad_hidden, up_w[k], NT)
        return carry

    lax.fori_loop(0, chunks, up_back_step, 0)
    for k in range(4):
        finish(down_out(k))
        finish(up_copy(k))


def feed(where, visible, normed_low, normed, vectors, cotangent, ups, down, after=()):
    rows, width = normed.shape
    chunks = 4
    part = sds((4, 4, width // 8, width), BF16)
    deep = pltpu.VMEM((chunks, width, width), BF16)
    long = pltpu.VMEM((chunks, rows, width), BF16)
    parts = pltpu.VMEM((2,) + part.shape, BF16)
    args = [where, visible, normed_low, normed, vectors, cotangent, *ups[0], *ups[1], down]
    return call(
        feed_kernel,
        "feed",
        32,
        [
            part,
            part,
            sds((width, chunks * width), BF16),
            sds((rows, width), BF16),
            sds((rows, width), F32),
            sds((8, width), F32),
            sds((8, width), F32),
        ],
        args,
        "ssvvvv" + "a" * 5,
        [
            deep,
            deep,
            long,
            pltpu.VMEM((chunks, rows, width), F32),
            pltpu.VMEM((rows, width), F32),
            pltpu.VMEM((rows, width), BF16),
            parts,
            deep,
        ]
        + [pltpu.SemaphoreType.DMA((4,))]
        + [pltpu.SemaphoreType.DMA] * 3,
        after,
        "aaavvvv",
        large=MOST,
    )


def place_square(where, j, block, keep, send):
    share = block.shape[0] // 8
    core = where[2]
    for z in range(4):
        for side, target in ((core, keep), (1 - core, send)):
            line = pl.multiple_of(share * (2 * z + side), share)
            target[j, where[1] ^ z] = block[pl.ds(line, share), :]


def mix_back_kernel(
    grad_normed, unit, inverse, vectors, mixed, weights, grad_pre, out_grad, grad_mixed, sums
):
    width = grad_normed.shape[1]
    grad = grad_normed[...]
    units = unit[...]
    pre = norm_back(grad, units, inverse[...], vectors[4:5, :])
    grad_pre[...] = ALPHA * pre
    low = pre.astype(BF16)
    sums[0:1, :] = jnp.sum(grad * units, 0, keepdims=True)
    sums[1:2, :] = jnp.sum(grad, 0, keepdims=True)
    sums[2:3, :] = jnp.sum(low.astype(F32), 0, keepdims=True)
    sums[3:8, :] = jnp.zeros((5, width), F32)
    out_grad[...] = dot(mixed[...], low, TN).astype(BF16)
    grad_mixed[...] = dot(low, weights[0], NT).astype(BF16)


def mix_back(grad_normed, unit, inverse, vectors, mixed, weights, after=()):
    total, width = grad_normed.shape

    def run(*refs):
        mix_back_kernel(*refs[:6], *refs[6 + len(after) :])

    whole = lambda x: pl.BlockSpec(x.shape, lambda i: (0,) * len(x.shape))
    outs = [
        sds((total, width), F32),
        sds((width, width), BF16),
        sds((total, width), BF16),
        sds((8, width), F32),
    ]
    return pl.pallas_call(
        run,
        grid=(1,),
        in_specs=[whole(x) for x in (grad_normed, unit, inverse, vectors, mixed)]
        + [pl.BlockSpec((1, width, width), lambda i: (3, 0, 0))]
        + [ANY] * len(after),
        out_specs=[whole(x) for x in outs],
        out_shape=outs,
        compiler_params=params(),
        name="mix_back",
        cost_estimate=cost(6),
    )(grad_normed, unit, inverse, vectors, mixed, weights, *after)


def attend_back_kernel(
    where, grad_mixed, out_grad, picked, query, key, value, soft, position, gates, *refs
):
    keep, send, grad_query, grad_key, grad_value, grad_gate, gated_scores, sums = refs[-12:-4]
    queries, keys, values, block = refs[-4:]
    pairs, rows = position.shape[1:3]
    width = picked.shape[1]
    clip = pl.program_id(0)
    cut = pl.ds(pl.multiple_of(clip * rows, rows), rows)
    for pair in range(pairs):
        lanes = pl.ds(128 * pair, 128)
        weights = soft[0, pair]
        weights_low = weights.astype(BF16)
        back = two_heads(grad_mixed[:, lanes])
        grad_soft = dot(value[:, lanes], back, NT)
        grad_value[:, lanes] = dot(weights_low, back).astype(BF16)
        carried = jnp.sum(grad_soft * weights, 0, keepdims=True)
        low_scores = (weights * (grad_soft - carried)).astype(BF16)
        scores = low_scores.astype(F32)
        grad_key[:, lanes] = dot(low_scores, two_heads(query[:, lanes])).astype(BF16)
        grad_query[:, lanes] = (one_block(dot(low_scores, key[:, lanes], TN)) * 0.125).astype(BF16)
        gate = jnp.concatenate(
            [gates[0, 2 * pair : 2 * pair + 1, :], gates[0, 2 * pair + 1 : 2 * pair + 2, :]], 1
        )
        by_gate = jnp.sum(scores * position[0, pair].astype(F32), 0, keepdims=True)
        grad_gate[0, 2 * pair : 2 * pair + 1, :] = by_gate[:, :rows]
        grad_gate[0, 2 * pair + 1 : 2 * pair + 2, :] = by_gate[:, rows:]
        gated_scores[0, pair] = (scores * gate).astype(BF16)
    grad_gate[0, 2 * pairs :, :] = jnp.zeros((16 - 2 * pairs, rows), F32)
    queries[cut, :] = grad_query[...]
    keys[cut, :] = grad_key[...]
    values[cut, :] = grad_value[...]

    @pl.when(clip == pl.num_programs(0) - 1)
    def _():
        sums[0:1, :] = jnp.sum(queries[...].astype(F32), 0, keepdims=True)
        sums[1:2, :] = jnp.sum(values[...].astype(F32), 0, keepdims=True)
        sums[2:8, :] = jnp.zeros((6, width), F32)
        x = picked[...]
        for j, grad in enumerate((queries, keys, values)):
            block[...] = dot(x, grad[...], TN).astype(BF16)
            place_square(where, j, block, keep, send)
        place_square(where, 3, out_grad, keep, send)


def attend_back(
    where, grad_mixed, out_grad, picked, query, key, value, soft, position, gates, after=()
):
    clips, pairs, rows = position.shape[:3]
    total, width = picked.shape
    flat = sds((total, width), BF16)
    part = sds((4, 4, width // 8, width), BF16)
    whole = lambda *s: pl.BlockSpec(s, lambda c: (0,) * len(s))
    lines = pl.BlockSpec((rows, width), lambda c: (c, 0))
    square = pl.BlockSpec((1, pairs, rows, 2 * rows), lambda c: (c, 0, 0, 0))
    gate = pl.BlockSpec((1, 16, rows), lambda c: (c, 0, 0))
    return pl.pallas_call(
        attend_back_kernel,
        grid=(clips,),
        in_specs=[
            SMEM,
            lines,
            whole(width, width),
            whole(total, width),
            lines,
            lines,
            lines,
            square,
            square,
            gate,
        ]
        + [ANY] * len(after),
        out_specs=[
            whole(*part.shape),
            whole(*part.shape),
            lines,
            lines,
            lines,
            gate,
            square,
            whole(8, width),
        ],
        out_shape=[
            part,
            part,
            flat,
            flat,
            flat,
            sds((clips, 16, rows), F32),
            sds(position.shape, BF16),
            sds((8, width), F32),
        ],
        scratch_shapes=[pltpu.VMEM((total, width), BF16)] * 3
        + [pltpu.VMEM((width, width), BF16)],
        compiler_params=params(0, "arbitrary"),
        name="attend_back",
        cost_estimate=cost(15),
    )(
        where, grad_mixed, out_grad, picked, query, key, value, soft, position, gates, *after
    )


def table_kernel(order, visible, gated, out, select, picks):
    clips, pairs, rows = gated.shape[:3]
    heads, total = 2 * pairs, clips * rows
    for c in range(clips):
        select[:, c * rows : (c + 1) * rows] = one_hot(order, visible, c, rows, SPAN)
    out[...] = jnp.zeros_like(out)

    def pair_step(pair, carry):
        for half in range(2):
            for c in range(clips):
                cut = slice(c * rows, (c + 1) * rows)
                block = gated[c, pair, :, half * rows : (half + 1) * rows]
                picks[cut, :] = dot(block, select[:, cut], NT).astype(BF16)
            sums = dot(select[...], picks[...])
            base = None
            for k in range(16):
                parts = []
                for t in range(SPAN // 64):
                    part = None
                    for m in range(SPAN // 128):
                        column = (t + m) % (SPAN // 64)
                        if column < SPAN // 128:
                            line = 128 * m + 8 * k
                            block = sums[line : line + 8, 128 * column : 128 * column + 128]
                            part = block if part is None else part + block
                    parts.append(jnp.zeros((8, 128), F32) if part is None else part)
                line = jnp.concatenate(parts, 1)
                line = pltpu.roll(line, 2 * SPAN - 8 * k, 1) if k else line
                base = line if base is None else base + line
            level = base[0:1, :]
            for r in range(1, 8):
                level = level + pltpu.roll(base[r : r + 1, :], 2 * SPAN - r, 1)
            out[pl.ds(2 * pair + half, 1), :] = level
        return carry

    lax.fori_loop(0, pairs, pair_step, 0)


def table_levels(order, visible, gated, after=()):
    total = gated.shape[0] * gated.shape[2]
    return call(
        table_kernel,
        "table_back",
        12,
        sds((16, 2 * SPAN), F32),
        [order, visible, gated],
        "vsv",
        [pltpu.VMEM((SPAN, total), BF16), pltpu.VMEM((total, SPAN), BF16)],
        after,
        large=MOST,
    )


def tokens_kernel(
    order, visible, gate_scale, grad_pre, grad_query, grad_key, grad_value, weights, picked, first,
    second, grad_gate, gate_weight, tokens_grad, gate_sums, gate_mix, grad_picked
):
    clips, patches = tokens_grad.shape[:2]
    total, width = picked.shape
    rows = total // clips
    spread = gate_spread(gate_weight, width)
    scale = scale_lines(gate_scale, rows)
    logits = []
    by_scale = jnp.zeros((16, rows), F32)
    for c in range(clips):
        one, two, grad = first[c], second[c], grad_gate[c]
        by_scale += grad * one * two
        logits.append(
            jnp.concatenate(
                [
                    grad * (two * scale - 1.0) * one * (1.0 - one),
                    grad * one * scale * two * (1.0 - two),
                ],
                0,
            )
        )
    logits = jnp.concatenate(logits, 1)
    gate_sums[...] = jnp.zeros_like(gate_sums)
    gate_sums[0:8, 0:32] = dot(jnp.ones((8, total), F32), logits, NT, HIGHEST)
    gate_sums[0:8, 32:48] = dot(jnp.ones((8, rows), F32), by_scale, NT, HIGHEST)
    gate_mix[...] = dot(logits, picked[...].astype(F32), NN, HIGHEST)
    grad = (
        grad_pre[...]
        + dot(grad_query[...], weights[0], NT)
        + dot(grad_key[...], weights[1], NT)
        + dot(grad_value[...], weights[2], NT)
        + dot(logits, spread, TN, HIGHEST)
    )
    grad_picked[...] = grad.astype(BF16)
    for c in range(clips):
        tokens_grad[c] = dot(
            one_hot(order, visible, c, rows, patches), grad_picked[c * rows : (c + 1) * rows, :]
        ).astype(BF16)


def tokens_back(patches, args, after=()):
    order, visible, picked = args[0], args[1], args[8]
    clips = visible.shape[0]
    total, width = picked.shape
    return call(
        tokens_kernel,
        "tokens_back",
        11,
        [
            sds((clips, patches, width), BF16),
            sds((8, 128), F32),
            sds((32, width), F32),
        ],
        args,
        "vss" + "v" * 10,
        [pltpu.VMEM((total, width), BF16)],
        after,
        large=MOST,
    )


def small_grads_kernel(
    where, sums_feed, up_b_grad, sums_mix, sums_attend, levels, buckets, gate_sums, gate_mix,
    keep, send, blocks
):
    width = sums_feed.shape[1]
    share = width // 8
    vectors = jnp.concatenate(
        [
            sums_attend[0:2, :],
            sums_mix[2:3, :],
            sums_feed[2:3, :],
            sums_mix[0:2, :],
            sums_feed[0:2, :],
        ],
        0,
    )
    ids = lines_of((384, 2 * SPAN))
    onehot = jnp.where(ids == buckets[...], 1.0, 0.0)
    table = dot(levels[...], onehot, NT, HIGHEST)
    count = NUM_BUCKETS // 8
    mix = gate_mix[...]
    own = lanes_of((16, width)) // 64 == lines_of((16, width))
    gates = []
    for half in range(2):
        line = jnp.sum(jnp.where(own, mix[16 * half : 16 * half + 16], 0.0), 0, keepdims=True)
        total = line[:, 0:128]
        for t in range(1, width // 128):
            total += line[:, 128 * t : 128 * t + 128]
        total += pltpu.roll(total, 64, 1)
        gates.append(total)
    gates.append(gate_sums[0:1, :])
    gates.append(jnp.zeros((1, 128), F32))
    gates = jnp.concatenate(gates, 0)
    for w in range(8):
        turned = pltpu.roll(vectors, width - share * w, 1) if w else vectors
        chunk = up_b_grad[w // 2 : w // 2 + 1, :]
        lines = [turned[:, :128]]
        for j in range(4):
            turn = 4 * share * (w % 2) + share * j
            lines.append((pltpu.roll(chunk, width - turn, 1) if turn else chunk)[:, :128])
        lines.append(gates)
        turned = pltpu.roll(table, 384 - count * w, 1) if w else table
        blocks[w] = jnp.concatenate([jnp.concatenate(lines, 0), turned[:, :128]], 1)
    for z in range(4):
        keep[where[1] ^ z] = blocks[2 * z + where[2]]
        send[where[1] ^ z] = blocks[2 * z + 1 - where[2]]


def small_grads(where, sums_feed, up_b_grad, sums_mix, sums_attend, levels, gate_sums, gate_mix):
    buckets = jnp.asarray(relative_buckets()[None, :])
    part = sds((4, 16, 256), F32)
    return call(
        small_grads_kernel,
        "small_grads",
        4,
        [part, part],
        [where, sums_feed, up_b_grad, sums_mix, sums_attend, levels, buckets, gate_sums, gate_mix],
        "s" + "v" * 8,
        [pltpu.VMEM((8, 16, 256), F32)],
    )


def swap_wide(x, flip):
    size = lax.axis_size("wide")
    return lax.ppermute(x, "wide", [(i, i ^ flip) for i in range(size)])


def swap_narrow(x, flip):
    size = lax.axis_size("narrow")
    return lax.ppermute(x, "narrow", [(i, i ^ flip) for i in range(size)])


def column_of(quarter):
    return [swap_wide(quarter, 2 * k) for k in range(1, 4)]


def plane_of(part):
    return [swap_narrow(part, m) for m in range(1, 4)]


def trade(parts):
    return lax.all_to_all(parts, "narrow", 0, 0)


def both_cores(own, plane):
    return (own, plane), (swap_wide(own, 1), swap_wide(plane, 1))


def core_sum_kernel(keep, came, *refs):
    refs[-1][...] = (keep[...].astype(F32) + came[...].astype(F32)).astype(BF16)


def core_sum(keep, came, after=()):
    return call(
        core_sum_kernel, "core_sum", 4, sds(keep.shape, BF16), [keep, came], "vv", after=after
    )


def sum_four(a, b, c, d):
    return (a.astype(F32) + b.astype(F32)) + (c.astype(F32) + d.astype(F32))


def halves(small, width):
    high = small.astype(BF16).astype(F32)
    return widen(jnp.concatenate([high, small - high], 1), width).astype(BF16)


def whole_of(both, lanes):
    return both[:, :lanes] + both[:, lanes : 2 * lanes]


def plane_sum_kernel(parts, *refs):
    smalls, outs = refs[:-4], refs[-4:]
    share = parts.shape[2]
    for k, out in enumerate(outs):
        out[:share, :] = sum_four(*(parts[j, k] for j in range(4))).astype(BF16)
        if smalls:
            out[share:, :] = halves(smalls[0][k] + smalls[1][k], out.shape[1])


def plane_sum(parts, smalls=(), after=()):
    share, width = parts.shape[2:]
    share += sum(s.shape[1] for s in smalls[:1])
    out = [sds((share, width), BF16)] * 4
    args = [parts, *smalls]
    return call(plane_sum_kernel, "plane_sum", 30, out, args, "v" * len(args), after=after)


def up_parts_kernel(up, out):
    width = out.shape[2]
    for j in range(4):
        out[j] = up[:, j * width : (j + 1) * width]


def up_parts(up, width, after=()):
    share = up.shape[0]
    return call(
        up_parts_kernel, "up_parts", 0.01, sds((4, share, width), BF16), [up], "v", after=after
    )


def column_sum_kernel(a, b, c, d, out):
    out[...] = sum_four(a[...], b[...], c[...], d[...]).astype(BF16)


def column_sum(parts, after=()):
    out = [sds(parts[0].shape, BF16)]
    return call(column_sum_kernel, "column_sum", 20, out, parts, "vvvv", after=after)[0]


def square_sum_kernel(a, b, c, d, out):
    share = out.shape[0] - 16
    total = sum_four(a[...], b[...], c[...], d[...])
    out[:share, :] = total[:share].astype(BF16)
    out[share:, :] = halves(whole_of(total[share:], 256), out.shape[1])


def square_sum(parts, after=()):
    out = [sds(parts[0].shape, BF16)]
    return call(square_sum_kernel, "square_sum", 20, out, parts, "vvvv", after=after)[0]


def end_sum_kernel(ups, square, out):
    share = ups.shape[1]
    up = sum_four(*(ups[j] for j in range(4))).astype(BF16)
    for j in range(4):
        out[j, :share, :] = up
        out[j, share:, :] = square[...]


def end_sum(ups, square, after=()):
    share, width = ups.shape[1:]
    out = sds((4, share + square.shape[0], width), BF16)
    return call(end_sum_kernel, "end_sum", 2, out, [ups, square], "vv", after=after)


def last_kernel(where, *refs):
    ends, downs = refs[0], refs[1:5]
    query, key, value, out, up, down = refs[5:11]
    vectors = refs[11:20]
    table, gate_weight, gate_bias, gate_scale = refs[20:]
    share, width = query.shape
    for j, target in enumerate((query, key, value, out)):
        up[:, j * width : (j + 1) * width] = ends[j, :share].astype(F32)
        target[...] = ends[j, share : 2 * share].astype(F32)
        line = pl.multiple_of((where[0] ^ j) * share, share)
        down[pl.ds(line, share), :] = downs[j][...].astype(F32)
    small = whole_of(sum_four(*(ends[j, 2 * share :] for j in range(4))), 256)
    sums = small[:, :128]
    heads, count = table.shape
    table[...] = small[:heads, 128 : 128 + count]
    lines = [sums[i : i + 1, :share] for i in range(8)]
    up_b = jnp.concatenate(
        [sums[8 + j : 9 + j, :share] for j in range(4)], 1
    )
    query_b, value_b, out_b, down_b, gain1, shift1, gain2, shift2 = lines
    for target, line in zip(
        vectors, (query_b, value_b, out_b, up_b, down_b, gain1, shift1, gain2, shift2)
    ):
        target[...] = line.reshape(target.shape)
    logits, size = gate_weight.shape
    half = logits // 2
    gate_weight[...] = jnp.where(
        lines_of((logits, 128)) < half, sums[12:13, :], sums[13:14, :]
    )[:, :size]
    line = sums[14:15, :]
    at = lanes_of((1, 128))
    one = jnp.sum(jnp.where(at < 16, line, 0.0), 1, keepdims=True)
    two = jnp.sum(jnp.where((at >= 16) & (at < 32), line, 0.0), 1, keepdims=True)
    gate_bias[...] = jnp.where(at < half, one, two)[:, : 2 * half]
    gate_scale[...] = pltpu.roll(line, 96, 1)[:, :heads]


def last(where, ends, downs, heads, logits):
    share, width = downs[0].shape
    line = sds((1, share), F32)
    return call(
        last_kernel,
        "last",
        5,
        [sds((share, width), F32)] * 4
        + [sds((share, 4 * width), F32), sds((4 * share, width), F32)]
        + [line] * 3
        + [sds((4 * share,), F32)]
        + [line] * 5
        + [
            sds((heads, NUM_BUCKETS // 8), F32),
            sds((logits, width // heads), F32),
            sds((1, logits), F32),
            sds((1, heads), F32),
        ],
        [where, ends, *downs],
        "s" + "v" * 5,
    )


def body(
    tokens,
    patch_order,
    visible,
    query_weight,
    key_weight,
    value_weight,
    out_weight,
    up_weight,
    down_weight,
    query_bias,
    value_bias,
    out_bias,
    up_bias,
    down_bias,
    first_gain,
    first_shift,
    second_gain,
    second_shift,
    bias_table,
    gate_weight,
    gate_bias,
    gate_scale,
    cotangent,
):
    clips, patches, width = tokens.shape
    rows = cotangent.shape[1]
    heads = bias_table.shape[1]
    pairs = heads // 2
    total = clips * rows
    hidden = up_weight.shape[1]
    share = width // 8
    n_wide, n_narrow = lax.axis_size("wide"), lax.axis_size("narrow")
    fast = n_wide == 8 and n_narrow == 4
    me_wide, me_narrow = lax.axis_index("wide"), lax.axis_index("narrow")
    vectors = [
        query_bias, value_bias, out_bias, down_bias,
        first_gain, first_shift, second_gain, second_shift,
    ]
    squares = [query_weight, key_weight, value_weight, out_weight]
    gate_lines = gate_weight.T
    gather = lambda x: lax.all_gather(x, "wide", axis=0, tiled=True)

    if fast:
        where = jnp.stack([me_narrow, me_wide // 2, me_wide % 2]).astype(jnp.int32)
        own_square, square_quarter = first_blocks(
            squares, [v[None, :] for v in vectors], up_bias, bias_table.T
        )
        picked, first, second, gates = pick(
            patch_order, visible, gate_bias, gate_scale, tokens, gate_lines, rows, square_quarter
        )
        own_up, up_quarter = up_blocks(where, up_weight, width, (picked,))
        column, small, down_copy = first_column(
            square_quarter, column_of(square_quarter), down_weight, (own_up,)
        )
        down_w = gather(down_copy)
        smalls = (small, swap_wide(small, 1))
        up_arrived = column_of(up_quarter)
        square_plane = trade(column)
    else:
        where = jnp.zeros((3,), jnp.int32)
        picked, first, second, gates = pick(
            patch_order, visible, gate_bias, gate_scale, tokens, gate_lines, rows, tokens
        )
        fold = lambda x: x.reshape(4, 2, share, width).transpose(1, 0, 2, 3)
        pack = lambda x: [(c[0], jnp.swapaxes(c[1:], 0, 1)) for c in (x[0], x[1])]
        square_blocks = pack(jnp.stack([fold(gather(w)) for w in squares], 2))
        ups = jnp.split(gather(up_weight), 4, 1)
        up_pieces = pack(jnp.stack([fold(u) for u in ups], 2))
        down_w = gather(down_weight)
        lines = [gather(v).reshape(8, 1, share) for v in vectors]
        lines += [gather(up_bias).reshape(8, 4, share), jnp.zeros((8, 4, share), BF16)]
        lines = jnp.pad(jnp.concatenate(lines, 1), ((0, 0), (0, 0), (0, 128 - share)))
        table = gather(bias_table).reshape(8, -1, heads).transpose(0, 2, 1)
        table = jnp.pad(table, ((0, 0), (0, 16 - heads), (0, 128 - table.shape[2])))
        small = jnp.concatenate([lines, table], 2)
        small = jnp.pad(small, ((0, 0), (0, 0), (0, width - 256))).reshape(4, 2, 16, width)
        smalls = (small[:, 0], small[:, 1])

    position, lines = positions(
        where, patch_order, visible, smalls, clips, rows, pairs, width
    )
    if fast:
        square_plane = hold(square_plane, (lines,))
        square_blocks = both_cores(own_square, square_plane)
        column = up_column(up_arrived, (lines,))
        up_plane = trade(hold(column, (square_plane,)))
    query, key, value, soft, mixed, unit, inverse, normed, normed_low, weights = attend(
        where, visible, picked, gates, position, lines, *square_blocks
    )
    if fast:
        up_pieces = both_cores(own_up, hold(up_plane, (normed_low,)))
    down_keep, down_send, up_grad, output, grad_normed, up_b_grad, sums_feed = feed(
        where, visible, normed_low, normed, lines, cotangent.reshape(total, width),
        up_pieces, down_w.reshape(4, width, width),
    )
    grad_pre1, out_grad, grad_mixed, sums_mix = mix_back(
        grad_normed, unit, inverse, lines, mixed, weights
    )
    later = ()
    if fast:
        up_sum = lax.psum_scatter(up_grad, "wide", scatter_dimension=0, tiled=True)
        down_parts = core_sum(down_keep, swap_wide(down_send, 1), after=(grad_mixed,))
        later = (down_parts,)
    (
        square_keep, square_send, grad_query, grad_key, grad_value, grad_gate, gated, sums_attend,
    ) = attend_back(
        where, grad_mixed, out_grad, picked, query, key, value, soft, position, gates, later
    )
    levels = table_levels(patch_order, visible, gated)
    later = (levels,)
    if fast:
        square_parts = core_sum(square_keep, swap_wide(square_send, 1), after=(levels,))
        down_parts = plane_sum(trade(down_parts), after=(square_parts,))
        later = (down_parts[0],)
    tokens_grad, gate_sums, gate_mix = tokens_back(
        patches,
        [
            patch_order, visible, gate_scale, grad_pre1, grad_query, grad_key, grad_value, weights,
            picked, first, second, grad_gate, gate_lines,
        ],
        later,
    )
    small_keep, small_send = small_grads(
        where, sums_feed, up_b_grad, sums_mix, sums_attend, levels, gate_sums, gate_mix
    )

    if fast:
        spread = lambda parts: [parts[0]] + [swap_wide(parts[k], 2 * k) for k in range(1, 4)]
        up_part = up_parts(up_sum, width, (small_keep,))
        down_part = column_sum(spread(down_parts), (up_part,))
        smalls = (small_keep, hold(swap_wide(small_send, 1), (down_part,)))
        square_parts = plane_sum(trade(square_parts), smalls)
        downs = [down_part, *plane_of(down_part)]
        ups = trade(hold(up_part, (square_parts[0],)))
        ends = trade(end_sum(ups, square_sum(spread(square_parts))))
        ends = last(where, ends, downs, heads, gate_lines.shape[0])
        weight_grads, ends = ends[:6], ends[6:]
        vector_grads = [v.reshape(-1) for v in ends[:9]]
        table_grad, gate_weight_grad = ends[9].T, ends[10].T
        gate_bias_grad, gate_scale_grad = ends[11].reshape(-1), ends[12].reshape(-1)
    else:
        def reduce(x):
            x = lax.psum_scatter(x, "wide", scatter_dimension=0, tiled=True)
            return lax.psum(x, "narrow").astype(F32)

        def mine(x):
            part = x.shape[0] // n_wide
            return lax.dynamic_slice_in_dim(x, me_wide * part, part, 0)

        square = jnp.stack([square_keep, square_send], 2).reshape(4, width, width)
        down = jnp.stack([down_keep, down_send]).transpose(2, 0, 1, 3, 4).reshape(hidden, width)
        weight_grads = [reduce(square[j]) for j in range(4)]
        weight_grads += [reduce(up_grad), reduce(down)]
        small = jnp.stack([small_keep, small_send], 1).reshape(8, 16, 256)
        small = lax.psum(small, ("narrow", "wide"))
        lines = small[:, :8, :share].transpose(1, 0, 2).reshape(8, width)
        up_b_grad = small[:, 8:12, :share].reshape(-1)
        query_b, value_b, out_b, down_b, gain1, shift1, gain2, shift2 = lines
        vector_grads = [
            mine(v)
            for v in (query_b, value_b, out_b, up_b_grad, down_b, gain1, shift1, gain2, shift2)
        ]
        table = small[:, :heads, 128 : 128 + NUM_BUCKETS // 8].transpose(0, 2, 1)
        table_grad = mine(table.reshape(-1, heads))
        size, half = gate_weight.shape[0], gate_weight.shape[1] // 2
        gate_weight_grad = jnp.repeat(small[0, 12:14, :size].T, half, 1)
        gate_bias_grad = jnp.repeat(jnp.sum(small[0, 14, :32].reshape(2, 16), 1), half)
        gate_scale_grad = small[0, 14, 32 : 32 + heads]
    return (
        output.reshape(clips, rows, width),
        tokens_grad,
        *weight_grads,
        *vector_grads,
        table_grad,
        gate_weight_grad,
        gate_bias_grad,
        gate_scale_grad,
    )


def solution(mesh):
    split = P(("narrow", "wide"))
    shard = P("wide")
    in_specs = (split,) * 3 + (shard,) * 16 + (P(),) * 3 + (split,)
    out_specs = (split,) * 2 + (shard,) * 16 + (P(),) * 3
    return jax.shard_map(body, mesh=mesh, in_specs=in_specs, out_specs=out_specs, check_vma=False)
```
